32 devices in a mesh: cfg: 2 (over y), row: 4 (over z), col: 4 (over x, core).
Axes of the slice: x: 2, y: 2, z: 4, core: 2. Of those that a mesh axis runs over, the one named last changes fastest.
Arguments:
- sigma_top: bfloat16 [8192, 4096], P(('cfg', 'row'), 'col'), parts along dimension 0, as said below
- par_panel: bfloat16 [8, 4, 6, 128, 128], P(('cfg', 'row'), 'col'), parts along dimension 0, may hold values from -0.03125 to 0.03125
- par_list: int32 [8, 4, 6], P(('cfg', 'row')), parts along dimension 0, may hold values from 0 to 7, as said below
- child_panel: bfloat16 [16, 4, 3, 128, 128], P(('cfg', 'row'), 'col'), parts along dimension 0, may hold values from -0.046875 to 0.046875
- child_top: bfloat16 [16, 128, 128], P(('cfg', 'row')), parts along dimension 0, may hold values from -0.625 to 0.625
- child_list: int32 [16, 4, 3], P(('cfg', 'row')), parts along dimension 0, may hold values from 0 to 5, as said below
- par_inv: float32 [8, 128, 128], P(('cfg', 'row')), parts along dimension 0, as said below
- child_inv: float32 [16, 128, 128], P(('cfg', 'row')), parts along dimension 0, as said below
Outputs:
- par_column: bfloat16 [8, 4, 6, 128, 128], P(('cfg', 'row'), 'col'), parts along dimension 0
- par_var: float32 [8, 128], P(('cfg', 'row')), parts along dimension 0
- child_column: bfloat16 [16, 4, 3, 128, 128], P(('cfg', 'row'), 'col'), parts along dimension 0
- child_row: bfloat16 [16, 128, 128], P(('cfg', 'row')), parts along dimension 0
- child_var: float32 [16, 128], P(('cfg', 'row')), parts along dimension 0
The draws below stay inside these ranges and needn't reach their ends.
There are 2 independent parts, one for each index of `cfg`. The reference program is written for one: setup_inputs(seed, part) draws one part's arguments, and reference() takes and returns one part's arrays. A program takes and returns all parts, laid end to end along the dimension named above; each array names one. Nothing has to cross between parts.
Inputs may be any that keep to these rules, and one draw needn't show every extreme that they name: `sigma_top`: symmetric. `par_list`: for each parent and group, 6 distinct increasing indices within the group. `child_list`: for each child and group, 3 distinct increasing slots of its parent's list in that group. `par_inv`: lower triangular. `child_inv`: lower triangular.
All inputs are finite; a program needn't handle non-finite values.
Results may differ from the reference program's by a relative error of at most 0.0052.
Values may be sent and summed in bfloat16 or wider, within the bound.
A program may use at most 64 MiB of HBM per device.

```python
import math
import jax
import jax.numpy as jnp
from jax import lax

B = 128
NA = 32
Q = 6
QC = 3
NG = 4
GB = 8
NP = 4
NCH = 8


def triangle(lower_values, diag_values):
    count = lower_values.shape[-1]
    below = (jnp.arange(count)[:, None] > jnp.arange(count)[None, :]).astype(jnp.float32)
    on_diag = (jnp.arange(count)[:, None] == jnp.arange(count)[None, :]).astype(jnp.float32)
    return lower_values * below + diag_values[..., None] * on_diag


def draw_sigma_top(key, part):
    key = jax.random.fold_in(key, 11)
    order = NA * B
    noise = jax.random.normal(key, (order, order), jnp.float32)
    symmetric = (noise + noise.T) * (0.3 / math.sqrt(2.0 * order))
    on_diag = (jnp.arange(order)[:, None] == jnp.arange(order)[None, :]).astype(jnp.float32)
    matrix = on_diag + symmetric
    matrix = matrix * 64.0
    return matrix.astype(jnp.bfloat16)


def draw_par_inv(key, part):
    key = jax.random.fold_in(key, 12)
    diag_key = jax.random.fold_in(key, 1)
    lower_values = jax.random.normal(key, (NP, B, B), jnp.float32) * (0.5 * B ** (-0.5))
    diag_values = jnp.exp(jax.random.uniform(diag_key, (NP, B), jnp.float32, math.log(0.5), math.log(1.5)))
    return triangle(lower_values, diag_values)


def draw_child_inv(key, part):
    key = jax.random.fold_in(key, 13)
    diag_key = jax.random.fold_in(key, 1)
    lower_values = jax.random.normal(key, (NCH, B, B), jnp.float32) * (0.5 * B ** (-0.5))
    diag_values = jnp.exp(jax.random.uniform(diag_key, (NCH, B), jnp.float32, math.log(0.5), math.log(1.5)))
    return triangle(lower_values, diag_values)


def draw_par_list(key, part):
    key = jax.random.fold_in(key, 14)
    scores = jax.random.randint(key, (NP, NG, GB), 0, 1 << 20) * GB + jnp.arange(GB, dtype=jnp.int32)
    chosen = jnp.argsort(scores, axis=-1)[..., :Q]
    return jnp.sort(chosen, axis=-1).astype(jnp.int32)


def draw_child_list(key, part):
    key = jax.random.fold_in(key, 15)
    scores = jax.random.randint(key, (NCH, NG, Q), 0, 1 << 20) * Q + jnp.arange(Q, dtype=jnp.int32)
    chosen = jnp.argsort(scores, axis=-1)[..., :QC]
    return jnp.sort(chosen, axis=-1).astype(jnp.int32)


def shard_levels(own_key, extent, split, least, top_value):
    def one(axis_at, blocks):
        draws = jax.random.uniform(jax.random.fold_in(jax.random.fold_in(own_key, 6), axis_at), (blocks,), jnp.float32, least / len(split), top_value / len(split))
        return jnp.repeat(jnp.exp(draws), extent[axis_at] // blocks).reshape((-1,) + (1,) * (len(extent) - axis_at - 1))

    gain = one(*split[0])
    for cut in split[1:]:
        gain = gain * one(*cut)
    return gain


def scatter_about(own_key, dims, deviation, most, cuts=(), kind=jnp.bfloat16):
    gain = shard_levels(own_key, dims, cuts, -0.22, 0.18) if cuts else 1.0
    array = jax.random.normal(own_key, dims, jnp.float32) * deviation * gain
    return jnp.minimum(jnp.maximum(array, -most), most).astype(kind)


def setup_inputs(seed: int = 0, part: int = 0) -> dict:
    seeds = jax.random.split(jax.random.key(seed), 9)
    part_splits = jax.random.split(jax.random.fold_in(seeds[8], part), 9)
    sigma_top = draw_sigma_top(jax.random.fold_in(jax.random.fold_in(seeds[8], part), 71), part)
    par_panel = scatter_about(part_splits[1], (NP, NG, Q, B, B), (0.125 * (NG * Q * B) ** -0.5), 0.03125, ((0, 4), (1, 4)))
    par_list = draw_par_list(jax.random.fold_in(jax.random.fold_in(seeds[8], part), 71), part)
    child_panel = scatter_about(part_splits[3], (NCH, NG, QC, B, B), (0.125 * (NG * QC * B) ** -0.5), 0.046875, ((0, 4), (1, 4)))
    child_top = scatter_about(part_splits[4], (NCH, B, B), (0.5 * B ** -0.5), 0.625, ((0, 4),))
    child_list = draw_child_list(jax.random.fold_in(jax.random.fold_in(seeds[8], part), 71), part)
    par_inv = draw_par_inv(jax.random.fold_in(jax.random.fold_in(seeds[8], part), 71), part)
    child_inv = draw_child_inv(jax.random.fold_in(jax.random.fold_in(seeds[8], part), 71), part)
    return dict(sigma_top=sigma_top, par_panel=par_panel, par_list=par_list, child_panel=child_panel, child_top=child_top, child_list=child_list, par_inv=par_inv, child_inv=child_inv)


PRECISE = lax.Precision.HIGHEST


def group_partials(sig_blocks, block_index, panel):
    count = block_index.shape[1]
    flat_index = block_index.reshape(-1)
    row_blocks = jnp.take(sig_blocks, flat_index, axis=0)
    sub_blocks = jnp.take(row_blocks, flat_index, axis=2).astype(jnp.float32)
    sub_blocks = sub_blocks.reshape(NG * count, B, NG, count, B)
    partial_value = jnp.einsum('ibhqk,hqkn->hibn', sub_blocks, panel.astype(jnp.float32), precision=PRECISE)
    rounded = lax.optimization_barrier(partial_value.astype(jnp.bfloat16))
    return jnp.sum(rounded.astype(jnp.float32), axis=0).reshape(NG, count, B, B)


def reference(sigma_top, par_panel, par_list, child_panel, child_top, child_list, par_inv, child_inv):
    sig_blocks = sigma_top.reshape(NA, B, NA, B)
    offsets = (jnp.arange(NG, dtype=jnp.int32) * GB)[:, None]
    par_blocks = (par_list + offsets[None]).astype(jnp.int32)
    par_sum = lax.map(lambda pair_args: group_partials(sig_blocks, pair_args[0], pair_args[1]), (par_blocks, par_panel))
    par_column = (-par_sum).astype(jnp.bfloat16)
    par_col_wide = par_column.astype(jnp.float32)
    par_gram = jnp.einsum('pji,pjk->pik', par_inv, par_inv, precision=PRECISE)
    par_cov = par_gram - jnp.einsum('pgqki,pgqkn->pin', par_panel.astype(jnp.float32), par_col_wide, precision=PRECISE)
    par_var = jnp.diagonal(par_cov, axis1=1, axis2=2)
    parent_of = jnp.arange(NCH, dtype=jnp.int32) // 2
    child_blocks = jnp.take_along_axis(par_blocks[parent_of], child_list, axis=2).astype(jnp.int32)
    child_sum = lax.map(lambda pair_args: group_partials(sig_blocks, pair_args[0], pair_args[1]), (child_blocks, child_panel))
    parent_sel = jnp.take_along_axis(par_col_wide[parent_of], child_list[:, :, :, None, None], axis=2)
    top_wide = child_top.astype(jnp.float32)
    child_pan_wide = child_panel.astype(jnp.float32)
    upper_rows = child_sum + jnp.einsum('cgsbk,ckn->cgsbn', parent_sel, top_wide, precision=PRECISE)
    child_column = (-upper_rows).astype(jnp.bfloat16)
    parent_rows = jnp.einsum('cgski,cgskn->cin', parent_sel, child_pan_wide, precision=PRECISE)
    parent_rows = parent_rows + jnp.einsum('cik,ckn->cin', par_cov[parent_of], top_wide, precision=PRECISE)
    child_row = (-parent_rows).astype(jnp.bfloat16)
    child_gram = jnp.einsum('cji,cjk->cik', child_inv, child_inv, precision=PRECISE)
    child_cov = child_gram - jnp.einsum('cgski,cgskn->cin', child_pan_wide, child_column.astype(jnp.float32), precision=PRECISE)
    child_cov = child_cov + jnp.einsum('cki,ckn->cin', top_wide, parent_rows, precision=PRECISE)
    child_var = jnp.diagonal(child_cov, axis1=1, axis2=2)
    return par_column, par_var, child_column, child_row, child_var
```

```python
import functools

import jax
import jax.numpy as jnp
from jax import lax
from jax.experimental import pallas as pl
from jax.experimental.pallas import tpu as pltpu
from jax.sharding import PartitionSpec as P

PRECISE = lax.Precision.HIGHEST


def densify(onehot_table, panel):
    spread = jnp.einsum("kqg,kqbn->gbkn", onehot_table, panel, preferred_element_type=jnp.float32)
    return spread.astype(jnp.bfloat16)


def on_device(
    sigma_top, par_panel, par_list, child_panel, child_top, child_list, par_inv, child_inv
):
    col_group = lax.axis_index("col")
    n_parents = par_panel.shape[0]
    n_children = child_panel.shape[0]
    block_width = par_panel.shape[-1]
    n_groups = par_list.shape[1]
    group_blocks = sigma_top.shape[1] // block_width
    total_blocks = n_groups * group_blocks
    slot_count = par_list.shape[2]
    child_count = child_list.shape[2]
    n_panels = n_parents + n_children
    parent_of = jnp.arange(n_children, dtype=jnp.int32) // 2
    par_here = lax.dynamic_index_in_dim(par_list, col_group, 1, keepdims=False)
    child_here = lax.dynamic_index_in_dim(child_list, col_group, 1, keepdims=False)
    child_local = jnp.take_along_axis(par_here[parent_of], child_here, axis=1)
    block_grid = jnp.arange(group_blocks, dtype=jnp.int32)
    par_onehot = (par_here[:, :, None] == block_grid).astype(jnp.bfloat16)
    child_onehot = (child_local[:, :, None] == block_grid).astype(jnp.bfloat16)
    dense_panels = jnp.concatenate(
        [densify(par_onehot, par_panel[:, 0]), densify(child_onehot, child_panel[:, 0])], axis=2
    )
    dense_panels = dense_panels.reshape(group_blocks * block_width, n_panels * block_width)
    products = jnp.dot(
        lax.all_gather(sigma_top, "row", axis=0, tiled=True),
        dense_panels,
        preferred_element_type=jnp.float32,
    ).astype(jnp.bfloat16)
    product_blocks = products.reshape(total_blocks, block_width, n_panels, block_width)
    offsets = (jnp.arange(n_groups, dtype=jnp.int32) * group_blocks)[:, None]
    par_blocks = par_list + offsets[None]
    child_blocks = jnp.take_along_axis(par_blocks[parent_of], child_list, axis=2)

    def pick_blocks(block_index, column):
        found_rows = jnp.take(product_blocks, block_index.reshape(-1), axis=0)
        return lax.dynamic_index_in_dim(found_rows, column, 2, keepdims=False)

    par_partial = jax.vmap(pick_blocks)(par_blocks, jnp.arange(n_parents, dtype=jnp.int32))
    par_partial = par_partial.reshape(n_parents, n_groups, slot_count, block_width, block_width)
    child_partial = jax.vmap(pick_blocks)(
        child_blocks, n_parents + jnp.arange(n_children, dtype=jnp.int32)
    )
    child_partial = child_partial.reshape(
        n_children, n_groups, child_count, block_width, block_width
    )
    par_gram = jnp.einsum("pji,pjk->pik", par_inv, par_inv, precision=PRECISE)
    child_gram = jnp.einsum("cji,cjk->cik", child_inv, child_inv, precision=PRECISE)
    top_wide = child_top.astype(jnp.float32)
    par_recv, child_recv = (
        lax.all_to_all(par_partial, "col", split_axis=1, concat_axis=1, tiled=True),
        lax.all_to_all(child_partial, "col", split_axis=1, concat_axis=1, tiled=True),
    )
    par_sum = jnp.sum(par_recv.astype(jnp.float32), axis=1, keepdims=True)
    child_sum = jnp.sum(child_recv.astype(jnp.float32), axis=1, keepdims=True)
    par_column = (-par_sum).astype(jnp.bfloat16)
    par_col_wide = par_column[:, 0].astype(jnp.float32)
    parent_sel = jnp.take_along_axis(par_col_wide[parent_of], child_here[:, :, None, None], axis=1)
    upper_rows = child_sum[:, 0] + jnp.einsum(
        "csbk,ckn->csbn", parent_sel, top_wide, precision=PRECISE
    )
    child_column = (-upper_rows).astype(jnp.bfloat16)[:, None]
    child_pan_wide = child_panel[:, 0].astype(jnp.float32)
    par_piece = jnp.einsum(
        "pqki,pqkn->pin", par_panel[:, 0].astype(jnp.float32), par_col_wide, precision=PRECISE
    )
    row_piece = jnp.einsum("cski,cskn->cin", parent_sel, child_pan_wide, precision=PRECISE)
    child_piece = jnp.einsum(
        "cski,cskn->cin", child_pan_wide, child_column[:, 0].astype(jnp.float32), precision=PRECISE
    )
    par_total, row_total = lax.psum((par_piece, row_piece), "col")
    par_cov = par_gram - par_total
    parent_rows = row_total + jnp.einsum(
        "cik,ckn->cin", par_cov[parent_of], top_wide, precision=PRECISE
    )
    child_total = lax.psum(child_piece.astype(jnp.bfloat16), "col").astype(jnp.float32)
    child_cov = (
        child_gram
        - child_total
        + jnp.einsum("cki,ckn->cin", top_wide, parent_rows, precision=PRECISE)
    )
    par_var = jnp.diagonal(par_cov, axis1=1, axis2=2)
    child_row = (-parent_rows).astype(jnp.bfloat16)
    child_var = jnp.diagonal(child_cov, axis1=1, axis2=2)
    return (par_column, par_var, child_column, child_row, child_var)


ROWS = 4
COLS = 4
LANES = 128


def transposed_dot(a, b, precision=None):
    return lax.dot_general(
        a, b, (((0,), (0,)), ((), ())), preferred_element_type=jnp.float32, precision=precision
    )


def fused_kernel(
    slots,
    picks,
    kids,
    sig,
    ppan,
    cpan,
    top,
    lst,
    pinv,
    cinv,
    pcol,
    pvar,
    ccol,
    crow,
    cvar,
    pan_all,
    own_part,
    sib_part,
    pair_sum,
    z_recv,
    x_recv,
    list_all,
    dense,
    dense_out,
    tail_recv,
    in_send,
    in_recv,
    lst_send,
    lst_recv,
    sib_send,
    sib_recv,
    z_send,
    z_recv_sem,
    x_send,
    x_recv_sem,
    tail_send,
    tail_recv_sem,
):
    width = LANES
    blocks = slots + kids * picks
    z = lax.axis_index("row")
    col = lax.axis_index("col")
    core = lax.rem(col, 2)
    xpos = lax.div(col, 2)
    chip = xpos * 2
    sibling = chip + 1 - core
    across = (1 - xpos) * 2 + core

    def remote(src, dst, send, recv, row, column):
        return pltpu.make_async_remote_copy(
            src_ref=src,
            dst_ref=dst,
            send_sem=send,
            recv_sem=recv,
            device_id={"row": row, "col": column},
            device_id_type=pl.DeviceIdType.MESH,
        )

    def visit(t):
        p = jnp.int32(0)
        for zz in range(ROWS):
            nearest = sorted(range(ROWS), key=lambda q: (abs(q - zz), (q < zz) == (zz >= 2)))
            for tt in range(ROWS):
                p = jnp.where((z == zz) & (t == tt), nearest[tt], p)
        return p

    barrier = pltpu.get_barrier_semaphore()
    for step in range(1, ROWS):
        for k in range(2):
            pl.semaphore_signal(
                barrier,
                inc=1,
                device_id={"row": lax.rem(z + step, ROWS), "col": chip + k},
                device_id_type=pl.DeviceIdType.MESH,
            )
    pl.semaphore_signal(
        barrier, inc=1, device_id={"row": z, "col": sibling}, device_id_type=pl.DeviceIdType.MESH
    )
    for k in range(2):
        pl.semaphore_signal(
            barrier,
            inc=1,
            device_id={"row": z, "col": (1 - xpos) * 2 + k},
            device_id_type=pl.DeviceIdType.MESH,
        )
    pl.semaphore_wait(barrier, 2 * ROWS + 1)

    own_parts = (ppan, cpan)
    bounds = ((0, slots), (slots, kids * picks))

    def list_copy(step):
        target = lax.rem(z + step, ROWS)
        return remote(
            lst.at[0], list_all.at[z], lst_send.at[target], lst_recv.at[z], target, col
        )

    def list_arrival(p):
        return remote(lst.at[0], list_all.at[p], lst_send.at[p], lst_recv.at[p], p, col)

    def panel_part(p, part):
        first, count = bounds[part]
        return pan_all.at[p, pl.ds(first, count)]

    def own_copy(part, up):
        return remote(
            own_parts[part],
            panel_part(z, part),
            in_send.at[up, z, part],
            in_recv.at[z, part],
            z + 1 if up else z - 1,
            col,
        )

    def forward(p, part, up):
        return remote(
            panel_part(p, part),
            panel_part(p, part),
            in_send.at[up, p, part],
            in_recv.at[p, part],
            z + 1 if up else z - 1,
            col,
        )

    for step in range(1, ROWS):
        list_copy(step).start()
    for part in range(2):

        @pl.when(z < ROWS - 1)
        def _():
            own_copy(part, 1).start()

        @pl.when(z > 0)
        def _():
            own_copy(part, 0).start()

    for part in range(2):
        first, count = bounds[part]
        pan_all[z, pl.ds(first, count)] = own_parts[part][...]
    list_all[z] = lst[0]

    def sib_copy(p):
        slot = lax.div(p, 2)
        return remote(
            own_part.at[p], sib_part.at[slot], sib_send.at[slot], sib_recv.at[slot], z, sibling
        )

    def z_copy(p):
        slot = lax.div(p, 2)
        here = lax.div(z, 2)
        return remote(
            pair_sum.at[slot],
            z_recv.at[here],
            z_send.at[slot],
            z_recv_sem.at[here],
            p,
            chip + lax.rem(z, 2),
        )

    group_blocks = sig.shape[1] // width
    spans = [(q, group_blocks - slots + q + 1) for q in range(slots)]
    spans += [
        (s, group_blocks - picks + s + 1) for _ in range(kids) for s in range(picks)
    ]
    panel_of = [0] * slots + [1 + kid for kid in range(kids) for _ in range(picks)]

    def places(table):
        table = table.astype(jnp.float32)
        return [jnp.broadcast_to(table[e : e + 1], (width, width)) for e in range(blocks)]

    @pl.loop(0, ROWS + 1)
    def _(t):
        @pl.when(t < ROWS)
        def _():
            p = visit(t)

            @pl.when(p != z)
            def _():
                for part in range(2):
                    forward(p, part, 0).wait_recv()

                    @pl.when((p < z) & (z < ROWS - 1))
                    def _():
                        forward(p, part, 1).start()

                    @pl.when((p > z) & (z > 0))
                    def _():
                        forward(p, part, 0).start()

                list_arrival(p).wait_recv()

            at = places(list_all[p, col])
            for panel in range(1 + kids):
                entries = [e for e in range(blocks) if panel_of[e] == panel]
                for b in range(group_blocks):
                    value = jnp.zeros((width, width), jnp.float32)
                    for e in entries:
                        if spans[e][0] <= b < spans[e][1]:
                            value = jnp.where(at[e] == b, pan_all[p, e].astype(jnp.float32), value)
                    dense[pl.ds(b * width, width), pl.ds(panel * width, width)] = value.astype(
                        jnp.bfloat16
                    )
            dense_out[...] = jnp.dot(sig[...], dense[...], preferred_element_type=jnp.float32)
            at = places(list_all[p, z])
            for e in range(blocks):
                first, end = spans[e]
                lane = pl.ds(panel_of[e] * width, width)
                value = dense_out[pl.ds(first * width, width), lane]
                for b in range(first + 1, end):
                    value = jnp.where(
                        at[e] == b, dense_out[pl.ds(b * width, width), lane], value
                    )
                own_part[p, e] = value.astype(jnp.bfloat16)

            @pl.when(lax.rem(p, 2) != core)
            def _():
                sib_copy(p).start()

        @pl.when(t > 0)
        def _():
            p = visit(t - 1)

            @pl.when(lax.rem(p, 2) == core)
            def _():
                slot = lax.div(p, 2)
                sib_copy(p).wait_recv()

                @pl.loop(0, blocks)
                def _(b):
                    total = own_part[p, b].astype(jnp.float32) + sib_part[slot, b].astype(
                        jnp.float32
                    )
                    pair_sum[slot, b] = total.astype(jnp.bfloat16)

                @pl.when(p == z)
                def _():
                    z_recv[slot] = pair_sum[slot]

                @pl.when(p != z)
                def _():
                    z_copy(p).start()

    precise = lax.Precision.HIGHEST
    gram = transposed_dot(pinv[...], pinv[...], precise)
    wide_top = [top[kid].astype(jnp.float32) for kid in range(kids)]
    gram_top = [
        jnp.dot(gram, wide, precision=precise, preferred_element_type=jnp.float32)
        for wide in wide_top
    ]

    def z_arrival(slot):
        source = core + 2 * slot
        return remote(
            pair_sum.at[slot],
            z_recv.at[slot],
            z_send.at[slot],
            z_recv_sem.at[slot],
            source,
            chip + lax.rem(z, 2),
        )

    x_copy = remote(z_recv.at[1 - xpos], x_recv, x_send, x_recv_sem, z, across)

    @pl.when(core + 2 * (1 - xpos) != z)
    def _():
        z_arrival(1 - xpos).wait_recv()

    x_copy.start()

    @pl.when(core + 2 * xpos != z)
    def _():
        z_arrival(xpos).wait_recv()

    x_copy.wait_recv()

    own_slots = places(lst[1, col])
    par_diag = jnp.zeros((1, width), jnp.float32)
    for q in range(slots):
        total = z_recv[xpos, q].astype(jnp.float32) + x_recv[q].astype(jnp.float32)
        column = (-total).astype(jnp.bfloat16)
        pcol[q] = column
        par_diag += jnp.sum(
            ppan[q].astype(jnp.float32) * column.astype(jnp.float32), axis=0, keepdims=True
        )
    par_piece = transposed_dot(
        ppan[...].reshape(slots * width, width), pcol[...].reshape(slots * width, width)
    )
    tail_recv[col, pl.ds(kids * width, 8)] = jnp.zeros((8, width), jnp.float32)
    tail_recv[col, pl.ds(kids * width, 1)] = par_diag
    for kid in range(kids):
        kid_diag = jnp.zeros((1, width), jnp.float32)
        selected = []
        for s in range(picks):
            value = pcol[s].astype(jnp.float32)
            for q in range(s + 1, slots - picks + s + 1):
                value = jnp.where(
                    own_slots[slots + kid * picks + s] == q, pcol[q].astype(jnp.float32), value
                )
            selected.append(value.astype(jnp.bfloat16))
        piece = transposed_dot(
            jnp.concatenate(selected, axis=0),
            cpan[pl.ds(kid * picks, picks)].reshape(picks * width, width),
        )
        piece = piece - jnp.dot(
            par_piece, wide_top[kid], precision=precise, preferred_element_type=jnp.float32
        )
        tail_recv[col, pl.ds(kid * width, width)] = piece
        for s in range(picks):
            at = kid * picks + s
            upper = (
                z_recv[xpos, slots + at].astype(jnp.float32)
                + x_recv[slots + at].astype(jnp.float32)
                + jnp.dot(selected[s], top[kid], preferred_element_type=jnp.float32)
            )
            column = (-upper).astype(jnp.bfloat16)
            ccol[at] = column
            kid_diag += jnp.sum(
                cpan[at].astype(jnp.float32) * column.astype(jnp.float32), axis=0, keepdims=True
            )
        tail_recv[col, pl.ds(kids * width + 1 + kid, 1)] = kid_diag

    def tail_copy(step):
        target = lax.rem(col + step, COLS)
        return remote(
            tail_recv.at[col],
            tail_recv.at[col],
            tail_send.at[target],
            tail_recv_sem.at[col],
            z,
            target,
        )

    def tail_arrival(source):
        return remote(
            tail_recv.at[source],
            tail_recv.at[source],
            tail_send.at[source],
            tail_recv_sem.at[source],
            z,
            source,
        )

    for step in range(1, COLS):
        tail_copy(step).start()
    for step in range(1, COLS):
        tail_arrival(lax.rem(col + step, COLS)).wait_recv()
    sums = [tail_recv[c, pl.ds(kids * width, 8)] for c in range(COLS)]
    diags = sums[0] + sums[1] + sums[2] + sums[3]
    pvar[...] = jnp.sum(pinv[...] * pinv[...], axis=0, keepdims=True) - diags[0:1]
    for kid in range(kids):
        part = [tail_recv[c, pl.ds(kid * width, width)] for c in range(COLS)]
        rows = part[0] + part[1] + part[2] + part[3] + gram_top[kid]
        crow[kid] = (-rows).astype(jnp.bfloat16)
        inv = cinv[kid]
        cvar[pl.ds(kid, 1), :] = (
            jnp.sum(inv * inv, axis=0, keepdims=True)
            - diags[1 + kid : 2 + kid]
            + jnp.sum(wide_top[kid] * rows, axis=0, keepdims=True)
        )

    for step in range(1, ROWS):
        list_copy(step).wait_send()
    for step in range(1, COLS):
        tail_copy(step).wait_send()
    for part in range(2):

        @pl.when(z < ROWS - 1)
        def _():
            own_copy(part, 1).wait_send()

        @pl.when(z > 0)
        def _():
            own_copy(part, 0).wait_send()

        for p in range(ROWS):

            @pl.when((p < z) & (z < ROWS - 1))
            def _():
                forward(p, part, 1).wait_send()

            @pl.when((p > z) & (z > 0))
            def _():
                forward(p, part, 0).wait_send()

    for slot in range(2):
        sib_copy(1 - core + 2 * slot).wait_send()

        @pl.when(core + 2 * slot != z)
        def _():
            z_copy(core + 2 * slot).wait_send()

    x_copy.wait_send()


def fits_kernel(
    mesh, sigma_top, par_panel, par_list, child_panel, child_top, child_list, par_inv, child_inv
):
    groups = par_list.shape[1]
    order = sigma_top.shape[1]
    return (
        mesh.shape["row"] == ROWS
        and mesh.shape["col"] == COLS
        and groups == COLS
        and sigma_top.shape[0] == order
        and par_panel.shape[0] == 1
        and par_panel.shape[-1] == LANES
        and child_panel.shape[0] <= 7
        and order * order <= 1 << 22
    )


def on_device_kernel(
    sigma_top, par_panel, par_list, child_panel, child_top, child_list, par_inv, child_inv
):
    slots = par_panel.shape[2]
    kids, _, picks = child_panel.shape[:3]
    width = LANES
    blocks = slots + kids * picks

    group_blocks = sigma_top.shape[1] // width
    par_here = par_list[0]
    hit = child_list[..., None] == jnp.arange(slots, dtype=jnp.int32)
    child_place = jnp.sum(jnp.where(hit, par_here[None, :, None, :], 0), axis=-1)
    pad = -blocks % 16

    def table(children):
        rows = jnp.moveaxis(children, 0, 1).reshape(COLS, kids * picks)
        rows = jnp.concatenate([par_here, rows], axis=1)
        return jnp.pad(rows, ((0, 0), (0, pad)))

    lists = jnp.stack([table(child_place), table(child_list)]).astype(jnp.bfloat16)
    lists = jnp.broadcast_to(lists[..., None], lists.shape + (LANES,))
    bf16, f32 = jnp.bfloat16, jnp.float32
    vmem = pl.BlockSpec(memory_space=pltpu.VMEM)
    dma = pltpu.SemaphoreType.DMA
    outs = pl.pallas_call(
        functools.partial(fused_kernel, slots, picks, kids),
        out_shape=(
            jax.ShapeDtypeStruct((slots, width, width), bf16),
            jax.ShapeDtypeStruct((1, width), f32),
            jax.ShapeDtypeStruct((kids * picks, width, width), bf16),
            jax.ShapeDtypeStruct((kids, width, width), bf16),
            jax.ShapeDtypeStruct((kids, width), f32),
        ),
        in_specs=[vmem] * 7,
        out_specs=[vmem] * 5,
        scratch_shapes=[
            pltpu.VMEM((ROWS, blocks, width, width), bf16),
            pltpu.VMEM((ROWS, blocks, width, width), bf16),
            pltpu.VMEM((2, blocks, width, width), bf16),
            pltpu.VMEM((2, blocks, width, width), bf16),
            pltpu.VMEM((2, blocks, width, width), bf16),
            pltpu.VMEM((blocks, width, width), bf16),
            pltpu.VMEM((ROWS, COLS, blocks + pad, LANES), bf16),
            pltpu.VMEM((group_blocks * width, (1 + kids) * width), bf16),
            pltpu.VMEM((group_blocks * width, (1 + kids) * width), f32),
            pltpu.VMEM((COLS, kids * width + 8, width), f32),
            dma((2, ROWS, 2)),
            dma((ROWS, 2)),
            dma((ROWS,)),
            dma((ROWS,)),
            dma((2,)),
            dma((2,)),
            dma((2,)),
            dma((2,)),
            dma,
            dma,
            dma((COLS,)),
            dma((COLS,)),
        ],
        compiler_params=pltpu.CompilerParams(
            collective_id=0, has_side_effects=True, vmem_limit_bytes=40 * 1024 * 1024
        ),
    )(
        sigma_top,
        par_panel.reshape(slots, width, width),
        child_panel.reshape(kids * picks, width, width),
        child_top,
        lists,
        par_inv.reshape(width, width),
        child_inv,
    )
    pcol, pvar, ccol, crow, cvar = outs
    return (
        pcol.reshape(par_panel.shape),
        pvar,
        ccol.reshape(child_panel.shape),
        crow,
        cvar,
    )


def solution(mesh):
    in_specs = (
        P(("cfg", "row"), "col"),
        P(("cfg", "row"), "col", None, None, None),
        P(("cfg", "row"), None, None),
        P(("cfg", "row"), "col", None, None, None),
        P(("cfg", "row"), None, None),
        P(("cfg", "row"), None, None),
        P(("cfg", "row"), None, None),
        P(("cfg", "row"), None, None),
    )
    out_specs = (
        P(("cfg", "row"), "col", None, None, None),
        P(("cfg", "row"), None),
        P(("cfg", "row"), "col", None, None, None),
        P(("cfg", "row"), None, None),
        P(("cfg", "row"), None),
    )
    def body(*args):
        if fits_kernel(mesh, *args):
            return on_device_kernel(*args)
        return on_device(*args)

    return jax.shard_map(
        body, mesh=mesh, in_specs=in_specs, out_specs=out_specs, check_vma=False
    )
```

```python
import functools

import jax
import jax.numpy as jnp
from jax import lax
from jax.experimental import pallas as pl
from jax.experimental.pallas import tpu as pltpu
from jax.sharding import PartitionSpec as P

PRECISE = lax.Precision.HIGHEST


def densify(onehot_table, panel):
    spread = jnp.einsum("kqg,kqbn->gbkn", onehot_table, panel, preferred_element_type=jnp.float32)
    return spread.astype(jnp.bfloat16)


def on_device(
    sigma_top, par_panel, par_list, child_panel, child_top, child_list, par_inv, child_inv
):
    col_group = lax.axis_index("col")
    n_parents = par_panel.shape[0]
    n_children = child_panel.shape[0]
    block_width = par_panel.shape[-1]
    n_groups = par_list.shape[1]
    group_blocks = sigma_top.shape[1] // block_width
    total_blocks = n_groups * group_blocks
    slot_count = par_list.shape[2]
    child_count = child_list.shape[2]
    n_panels = n_parents + n_children
    parent_of = jnp.arange(n_children, dtype=jnp.int32) // 2
    par_here = lax.dynamic_index_in_dim(par_list, col_group, 1, keepdims=False)
    child_here = lax.dynamic_index_in_dim(child_list, col_group, 1, keepdims=False)
    child_local = jnp.take_along_axis(par_here[parent_of], child_here, axis=1)
    block_grid = jnp.arange(group_blocks, dtype=jnp.int32)
    par_onehot = (par_here[:, :, None] == block_grid).astype(jnp.bfloat16)
    child_onehot = (child_local[:, :, None] == block_grid).astype(jnp.bfloat16)
    dense_panels = jnp.concatenate(
        [densify(par_onehot, par_panel[:, 0]), densify(child_onehot, child_panel[:, 0])], axis=2
    )
    dense_panels = dense_panels.reshape(group_blocks * block_width, n_panels * block_width)
    products = jnp.dot(
        lax.all_gather(sigma_top, "row", axis=0, tiled=True),
        dense_panels,
        preferred_element_type=jnp.float32,
    ).astype(jnp.bfloat16)
    product_blocks = products.reshape(total_blocks, block_width, n_panels, block_width)
    offsets = (jnp.arange(n_groups, dtype=jnp.int32) * group_blocks)[:, None]
    par_blocks = par_list + offsets[None]
    child_blocks = jnp.take_along_axis(par_blocks[parent_of], child_list, axis=2)

    def pick_blocks(block_index, column):
        found_rows = jnp.take(product_blocks, block_index.reshape(-1), axis=0)
        return lax.dynamic_index_in_dim(found_rows, column, 2, keepdims=False)

    par_partial = jax.vmap(pick_blocks)(par_blocks, jnp.arange(n_parents, dtype=jnp.int32))
    par_partial = par_partial.reshape(n_parents, n_groups, slot_count, block_width, block_width)
    child_partial = jax.vmap(pick_blocks)(
        child_blocks, n_parents + jnp.arange(n_children, dtype=jnp.int32)
    )
    child_partial = child_partial.reshape(
        n_children, n_groups, child_count, block_width, block_width
    )
    par_gram = jnp.einsum("pji,pjk->pik", par_inv, par_inv, precision=PRECISE)
    child_gram = jnp.einsum("cji,cjk->cik", child_inv, child_inv, precision=PRECISE)
    top_wide = child_top.astype(jnp.float32)
    par_recv, child_recv = (
        lax.all_to_all(par_partial, "col", split_axis=1, concat_axis=1, tiled=True),
        lax.all_to_all(child_partial, "col", split_axis=1, concat_axis=1, tiled=True),
    )
    par_sum = jnp.sum(par_recv.astype(jnp.float32), axis=1, keepdims=True)
    child_sum = jnp.sum(child_recv.astype(jnp.float32), axis=1, keepdims=True)
    par_column = (-par_sum).astype(jnp.bfloat16)
    par_col_wide = par_column[:, 0].astype(jnp.float32)
    parent_sel = jnp.take_along_axis(par_col_wide[parent_of], child_here[:, :, None, None], axis=1)
    upper_rows = child_sum[:, 0] + jnp.einsum(
        "csbk,ckn->csbn", parent_sel, top_wide, precision=PRECISE
    )
    child_column = (-upper_rows).astype(jnp.bfloat16)[:, None]
    child_pan_wide = child_panel[:, 0].astype(jnp.float32)
    par_piece = jnp.einsum(
        "pqki,pqkn->pin", par_panel[:, 0].astype(jnp.float32), par_col_wide, precision=PRECISE
    )
    row_piece = jnp.einsum("cski,cskn->cin", parent_sel, child_pan_wide, precision=PRECISE)
    child_piece = jnp.einsum(
        "cski,cskn->cin", child_pan_wide, child_column[:, 0].astype(jnp.float32), precision=PRECISE
    )
    par_total, row_total = lax.psum((par_piece, row_piece), "col")
    par_cov = par_gram - par_total
    parent_rows = row_total + jnp.einsum(
        "cik,ckn->cin", par_cov[parent_of], top_wide, precision=PRECISE
    )
    child_total = lax.psum(child_piece.astype(jnp.bfloat16), "col").astype(jnp.float32)
    child_cov = (
        child_gram
        - child_total
        + jnp.einsum("cki,ckn->cin", top_wide, parent_rows, precision=PRECISE)
    )
    par_var = jnp.diagonal(par_cov, axis1=1, axis2=2)
    child_row = (-parent_rows).astype(jnp.bfloat16)
    child_var = jnp.diagonal(child_cov, axis1=1, axis2=2)
    return (par_column, par_var, child_column, child_row, child_var)


ROWS = 4
COLS = 4
LANES = 128


def transposed_dot(a, b, precision=None):
    return lax.dot_general(
        a, b, (((0,), (0,)), ((), ())), preferred_element_type=jnp.float32, precision=precision
    )


def fused_kernel(
    slots,
    picks,
    kids,
    sig_hbm,
    ppan_hbm,
    cpan_hbm,
    top_hbm,
    pinv_hbm,
    cinv_hbm,
    par_s,
    child_s,
    pcol,
    pvar,
    ccol,
    crow,
    cvar,
    pan_all,
    own_part,
    sib_part,
    pair_sum,
    z_recv,
    x_recv,
    list_all,
    dense,
    dense_out,
    tail_recv,
    kid_recv,
    sig,
    top,
    pinv,
    cinv,
    table,
    local_sem,
    in_send,
    in_recv,
    lst_send,
    lst_recv,
    sib_send,
    sib_recv,
    z_send,
    z_recv_sem,
    x_send,
    x_recv_sem,
    tail_send,
    tail_recv_sem,
    kid_send,
    kid_recv_sem,
):
    width = LANES
    blocks = slots + kids * picks
    z = lax.axis_index("row")
    col = lax.axis_index("col")
    core = lax.rem(col, 2)
    xpos = lax.div(col, 2)
    chip = xpos * 2
    sibling = chip + 1 - core
    across = (1 - xpos) * 2 + core

    def remote(src, dst, send, recv, row, column):
        return pltpu.make_async_remote_copy(
            src_ref=src,
            dst_ref=dst,
            send_sem=send,
            recv_sem=recv,
            device_id={"row": row, "col": column},
            device_id_type=pl.DeviceIdType.MESH,
        )

    def visit(t):
        p = jnp.int32(0)
        for zz in range(ROWS):
            nearest = sorted(range(ROWS), key=lambda q: (abs(q - zz), (q < zz) == (zz >= 2)))
            for tt in range(ROWS):
                p = jnp.where((z == zz) & (t == tt), nearest[tt], p)
        return p

    bounds = ((0, slots), (slots, kids * picks))

    def panel_part(p, part):
        first, count = bounds[part]
        return pan_all.at[p, pl.ds(first, count)]

    loads = [
        pltpu.make_async_copy(src, dst, local_sem.at[i])
        for i, (src, dst) in enumerate(
            (
                (ppan_hbm, panel_part(z, 0)),
                (cpan_hbm, panel_part(z, 1)),
                (sig_hbm, sig),
                (top_hbm, top),
                (pinv_hbm, pinv),
                (cinv_hbm, cinv),
            )
        )
    ]
    for load in loads:
        load.start()

    barrier = pltpu.get_barrier_semaphore()
    for step in range(1, ROWS):
        for k in range(2):
            pl.semaphore_signal(
                barrier,
                inc=1,
                device_id={"row": lax.rem(z + step, ROWS), "col": chip + k},
                device_id_type=pl.DeviceIdType.MESH,
            )
    pl.semaphore_signal(
        barrier, inc=1, device_id={"row": z, "col": sibling}, device_id_type=pl.DeviceIdType.MESH
    )
    for k in range(2):
        pl.semaphore_signal(
            barrier,
            inc=1,
            device_id={"row": z, "col": (1 - xpos) * 2 + k},
            device_id_type=pl.DeviceIdType.MESH,
        )
    table[...] = jnp.zeros_like(table)
    for g in range(COLS):
        for q in range(slots):
            value = par_s[0, g, q].astype(jnp.float32)
            table[g, pl.ds(q, 1), :] = jnp.full((1, width), value, jnp.float32)
        for kid in range(kids):
            for pick in range(picks):
                slot = child_s[kid, g, pick]
                place = par_s[0, g, pick]
                for q in range(pick + 1, slots - picks + pick + 1):
                    place = jnp.where(slot == q, par_s[0, g, q], place)
                value = place.astype(jnp.float32)
                table[g, pl.ds(slots + kid * picks + pick, 1), :] = jnp.full(
                    (1, width), value, jnp.float32
                )
    list_all[z] = table[...].astype(jnp.bfloat16)
    pl.semaphore_wait(barrier, 2 * ROWS + 1)

    def list_copy(step):
        target = lax.rem(z + step, ROWS)
        return remote(
            list_all.at[z], list_all.at[z], lst_send.at[target], lst_recv.at[z], target, col
        )

    def list_arrival(p):
        return remote(list_all.at[p], list_all.at[p], lst_send.at[p], lst_recv.at[p], p, col)

    def forward(p, part, up):
        return remote(
            panel_part(p, part),
            panel_part(p, part),
            in_send.at[up, p, part],
            in_recv.at[p, part],
            z + 1 if up else z - 1,
            col,
        )

    def send_own(part):
        @pl.when(z < ROWS - 1)
        def _():
            forward(z, part, 1).start()

        @pl.when(z > 0)
        def _():
            forward(z, part, 0).start()

    for step in range(1, ROWS):
        list_copy(step).start()
    loads[0].wait()
    send_own(0)
    for load in loads[1:]:
        load.wait()

    def cut(ref, index, part):
        first, count = bounds[part]
        return ref.at[index, pl.ds(first, count)]

    def sib_copy(p, part):
        slot = lax.div(p, 2)
        return remote(
            cut(own_part, p, part),
            cut(sib_part, slot, part),
            sib_send.at[slot, part],
            sib_recv.at[slot, part],
            z,
            sibling,
        )

    def z_copy(p, part):
        slot = lax.div(p, 2)
        here = lax.div(z, 2)
        return remote(
            cut(pair_sum, slot, part),
            cut(z_recv, here, part),
            z_send.at[slot, part],
            z_recv_sem.at[here, part],
            p,
            chip + lax.rem(z, 2),
        )

    def z_arrival(slot, part):
        return remote(
            cut(pair_sum, slot, part),
            cut(z_recv, slot, part),
            z_send.at[slot, part],
            z_recv_sem.at[slot, part],
            core + 2 * slot,
            chip + lax.rem(z, 2),
        )

    def x_copy(part):
        first, count = bounds[part]
        return remote(
            cut(z_recv, 1 - xpos, part),
            x_recv.at[pl.ds(first, count)],
            x_send.at[part],
            x_recv_sem.at[part],
            z,
            across,
        )

    def send_across(part):
        @pl.when(core + 2 * (1 - xpos) != z)
        def _():
            z_arrival(1 - xpos, part).wait_recv()

        x_copy(part).start()

    def take_across(part):
        @pl.when(core + 2 * xpos != z)
        def _():
            z_arrival(xpos, part).wait_recv()

        x_copy(part).wait_recv()

    group_blocks = sig.shape[1] // width
    spans = [(q, group_blocks - slots + q + 1) for q in range(slots)]
    spans += [
        (s, group_blocks - picks + s + 1) for _ in range(kids) for s in range(picks)
    ]
    panel_of = [0] * slots + [1 + kid for kid in range(kids) for _ in range(picks)]

    def places(rows):
        rows = rows.astype(jnp.float32)
        return [jnp.broadcast_to(rows[e : e + 1], (width, width)) for e in range(blocks)]

    def compute(p, part):
        first_entry, count = bounds[part]
        mine = range(first_entry, first_entry + count)
        panels = sorted({panel_of[e] for e in mine})
        low, span = panels[0], len(panels)
        at = places(list_all[p, col])
        for panel in panels:
            entries = [e for e in mine if panel_of[e] == panel]
            for b in range(group_blocks):
                value = jnp.zeros((width, width), jnp.float32)
                for e in entries:
                    if spans[e][0] <= b < spans[e][1]:
                        value = jnp.where(at[e] == b, pan_all[p, e].astype(jnp.float32), value)
                dense[pl.ds(b * width, width), pl.ds(panel * width, width)] = value.astype(
                    jnp.bfloat16
                )
        lanes = pl.ds(low * width, span * width)
        dense_out[:, lanes] = jnp.dot(
            sig[...], dense[:, lanes], preferred_element_type=jnp.float32
        )
        at = places(list_all[p, z])
        for e in mine:
            first, end = spans[e]
            lane = pl.ds(panel_of[e] * width, width)
            value = dense_out[pl.ds(first * width, width), lane]
            for b in range(first + 1, end):
                value = jnp.where(at[e] == b, dense_out[pl.ds(b * width, width), lane], value)
            own_part[p, e] = value.astype(jnp.bfloat16)

    def combine(p, part):
        first, count = bounds[part]
        slot = lax.div(p, 2)
        sib_copy(p, part).wait_recv()

        @pl.loop(first, first + count)
        def _(b):
            total = own_part[p, b].astype(jnp.float32) + sib_part[slot, b].astype(jnp.float32)
            pair_sum[slot, b] = total.astype(jnp.bfloat16)

        @pl.when(p == z)
        def _():
            z_recv[slot, pl.ds(first, count)] = pair_sum[slot, pl.ds(first, count)]

        @pl.when(p != z)
        def _():
            z_copy(p, part).start()

    def stage(part):
        @pl.loop(0, ROWS + 1)
        def _(t):
            @pl.when(t < ROWS)
            def _():
                p = visit(t)

                @pl.when(p != z)
                def _():
                    forward(p, part, 0).wait_recv()

                    @pl.when((p < z) & (z < ROWS - 1))
                    def _():
                        forward(p, part, 1).start()

                    @pl.when((p > z) & (z > 0))
                    def _():
                        forward(p, part, 0).start()

                    if part == 0:
                        list_arrival(p).wait_recv()

                if part == 0:

                    @pl.when(t == 1)
                    def _():
                        send_own(1)

                compute(p, part)

                @pl.when(lax.rem(p, 2) != core)
                def _():
                    sib_copy(p, part).start()

            if part == 1:

                @pl.when(t == ROWS)
                def _():
                    send_across(0)

            @pl.when(t > 0)
            def _():
                p = visit(t - 1)

                @pl.when(lax.rem(p, 2) == core)
                def _():
                    combine(p, part)

    stage(0)
    stage(1)

    precise = lax.Precision.HIGHEST
    gram = transposed_dot(pinv[...], pinv[...], precise)
    wide_top = [top[kid].astype(jnp.float32) for kid in range(kids)]
    gram_top = [
        jnp.dot(gram, wide, precision=precise, preferred_element_type=jnp.float32)
        for wide in wide_top
    ]

    def spread(buffer, send, recv, source, target):
        return remote(
            buffer.at[source], buffer.at[source], send.at[target], recv.at[source], z, target
        )

    def send_to_columns(buffer, send, recv):
        for step in range(1, COLS):
            spread(buffer, send, recv, col, lax.rem(col + step, COLS)).start()

    def take_from_columns(buffer, send, recv):
        for step in range(1, COLS):
            source = lax.rem(col + step, COLS)
            spread(buffer, send, recv, source, source).wait_recv()

    take_across(0)
    par_diag = jnp.zeros((1, width), jnp.float32)
    for q in range(slots):
        total = z_recv[xpos, q].astype(jnp.float32) + x_recv[q].astype(jnp.float32)
        column = (-total).astype(jnp.bfloat16)
        pcol[q] = column
        par_diag += jnp.sum(
            pan_all[z, q].astype(jnp.float32) * column.astype(jnp.float32), axis=0, keepdims=True
        )
    par_piece = transposed_dot(
        pan_all[z, pl.ds(0, slots)].reshape(slots * width, width),
        pcol[...].reshape(slots * width, width),
    )
    tail_recv[col, pl.ds(kids * width, 8)] = jnp.broadcast_to(par_diag, (8, width))
    lifted = []
    for kid in range(kids):
        selected = []
        for s in range(picks):
            slot = jnp.full((width, width), child_s[kid, col, s], jnp.int32)
            value = pcol[s].astype(jnp.float32)
            for q in range(s + 1, slots - picks + s + 1):
                value = jnp.where(slot == q, pcol[q].astype(jnp.float32), value)
            selected.append(value.astype(jnp.bfloat16))
        chosen = jnp.concatenate(selected, axis=0)
        piece = transposed_dot(
            chosen,
            pan_all[z, pl.ds(slots + kid * picks, picks)].reshape(picks * width, width),
        )
        piece = piece - jnp.dot(
            par_piece, wide_top[kid], precision=precise, preferred_element_type=jnp.float32
        )
        tail_recv[col, pl.ds(kid * width, width)] = piece
        lifted.append(jnp.dot(chosen, top[kid], preferred_element_type=jnp.float32))
    send_across(1)
    send_to_columns(tail_recv, tail_send, tail_recv_sem)

    take_across(1)
    kid_diags = []
    for kid in range(kids):
        kid_diag = jnp.zeros((1, width), jnp.float32)
        for s in range(picks):
            at = kid * picks + s
            upper = (
                z_recv[xpos, slots + at].astype(jnp.float32)
                + x_recv[slots + at].astype(jnp.float32)
                + lifted[kid][s * width : (s + 1) * width]
            )
            column = (-upper).astype(jnp.bfloat16)
            ccol[at] = column
            kid_diag += jnp.sum(
                pan_all[z, slots + at].astype(jnp.float32) * column.astype(jnp.float32),
                axis=0,
                keepdims=True,
            )
        kid_diags.append(kid_diag)
    kid_diags.append(jnp.zeros((8 - kids, width), jnp.float32))
    kid_recv[col] = jnp.concatenate(kid_diags, axis=0)
    send_to_columns(kid_recv, kid_send, kid_recv_sem)

    take_from_columns(tail_recv, tail_send, tail_recv_sem)
    par_total = [tail_recv[c, pl.ds(kids * width, 8)][0:1] for c in range(COLS)]
    pvar[...] = jnp.sum(pinv[...] * pinv[...], axis=0, keepdims=True) - (
        par_total[0] + par_total[1] + par_total[2] + par_total[3]
    )
    known = []
    for kid in range(kids):
        part = [tail_recv[c, pl.ds(kid * width, width)] for c in range(COLS)]
        rows = part[0] + part[1] + part[2] + part[3] + gram_top[kid]
        crow[kid] = (-rows).astype(jnp.bfloat16)
        inv = cinv[kid]
        known.append(
            jnp.sum(inv * inv, axis=0, keepdims=True)
            + jnp.sum(wide_top[kid] * rows, axis=0, keepdims=True)
        )
    take_from_columns(kid_recv, kid_send, kid_recv_sem)
    kid_total = kid_recv[0] + kid_recv[1] + kid_recv[2] + kid_recv[3]
    for kid in range(kids):
        cvar[pl.ds(kid, 1), :] = known[kid] - kid_total[kid : kid + 1]

    for step in range(1, ROWS):
        list_copy(step).wait_send()
    for step in range(1, COLS):
        target = lax.rem(col + step, COLS)
        spread(tail_recv, tail_send, tail_recv_sem, col, target).wait_send()
        spread(kid_recv, kid_send, kid_recv_sem, col, target).wait_send()
    for part in range(2):
        for p in range(ROWS):

            @pl.when((p <= z) & (z < ROWS - 1))
            def _():
                forward(p, part, 1).wait_send()

            @pl.when((p >= z) & (z > 0))
            def _():
                forward(p, part, 0).wait_send()

        for slot in range(2):
            sib_copy(1 - core + 2 * slot, part).wait_send()

            @pl.when(core + 2 * slot != z)
            def _():
                z_copy(core + 2 * slot, part).wait_send()

        x_copy(part).wait_send()


def fits_kernel(
    mesh, sigma_top, par_panel, par_list, child_panel, child_top, child_list, par_inv, child_inv
):
    groups = par_list.shape[1]
    order = sigma_top.shape[1]
    return (
        mesh.shape["row"] == ROWS
        and mesh.shape["col"] == COLS
        and groups == COLS
        and sigma_top.shape[0] == order
        and par_panel.shape[0] == 1
        and par_panel.shape[-1] == LANES
        and child_panel.shape[0] <= 7
        and order * order <= 1 << 22
    )


def on_device_kernel(
    sigma_top, par_panel, par_list, child_panel, child_top, child_list, par_inv, child_inv
):
    slots = par_panel.shape[2]
    kids, _, picks = child_panel.shape[:3]
    width = LANES
    blocks = slots + kids * picks

    group_blocks = sigma_top.shape[1] // width
    pad = -blocks % 16
    bf16, f32 = jnp.bfloat16, jnp.float32
    vmem = pl.BlockSpec(memory_space=pltpu.VMEM)
    smem = pl.BlockSpec(memory_space=pltpu.SMEM)
    hbm = pl.BlockSpec(memory_space=pltpu.HBM)
    dma = pltpu.SemaphoreType.DMA
    outs = pl.pallas_call(
        functools.partial(fused_kernel, slots, picks, kids),
        out_shape=(
            jax.ShapeDtypeStruct((slots, width, width), bf16),
            jax.ShapeDtypeStruct((1, width), f32),
            jax.ShapeDtypeStruct((kids * picks, width, width), bf16),
            jax.ShapeDtypeStruct((kids, width, width), bf16),
            jax.ShapeDtypeStruct((kids, width), f32),
        ),
        in_specs=[hbm] * 6 + [smem] * 2,
        out_specs=[vmem] * 5,
        scratch_shapes=[
            pltpu.VMEM((ROWS, blocks, width, width), bf16),
            pltpu.VMEM((ROWS, blocks, width, width), bf16),
            pltpu.VMEM((2, blocks, width, width), bf16),
            pltpu.VMEM((2, blocks, width, width), bf16),
            pltpu.VMEM((2, blocks, width, width), bf16),
            pltpu.VMEM((blocks, width, width), bf16),
            pltpu.VMEM((ROWS, COLS, blocks + pad, LANES), bf16),
            pltpu.VMEM((group_blocks * width, (1 + kids) * width), bf16),
            pltpu.VMEM((group_blocks * width, (1 + kids) * width), f32),
            pltpu.VMEM((COLS, kids * width + 8, width), f32),
            pltpu.VMEM((COLS, 8, width), f32),
            pltpu.VMEM(sigma_top.shape, bf16),
            pltpu.VMEM(child_top.shape, bf16),
            pltpu.VMEM((width, width), f32),
            pltpu.VMEM(child_inv.shape, f32),
            pltpu.VMEM((COLS, blocks + pad, LANES), f32),
            dma((6,)),
            dma((2, ROWS, 2)),
            dma((ROWS, 2)),
            dma((ROWS,)),
            dma((ROWS,)),
            dma((2, 2)),
            dma((2, 2)),
            dma((2, 2)),
            dma((2, 2)),
            dma((2,)),
            dma((2,)),
            dma((COLS,)),
            dma((COLS,)),
            dma((COLS,)),
            dma((COLS,)),
        ],
        compiler_params=pltpu.CompilerParams(
            collective_id=0, has_side_effects=True, vmem_limit_bytes=40 * 1024 * 1024
        ),
    )(
        sigma_top,
        par_panel.reshape(slots, width, width),
        child_panel.reshape(kids * picks, width, width),
        child_top,
        par_inv.reshape(width, width),
        child_inv,
        par_list,
        child_list,
    )
    pcol, pvar, ccol, crow, cvar = outs
    return (
        pcol.reshape(par_panel.shape),
        pvar,
        ccol.reshape(child_panel.shape),
        crow,
        cvar,
    )


def solution(mesh):
    in_specs = (
        P(("cfg", "row"), "col"),
        P(("cfg", "row"), "col", None, None, None),
        P(("cfg", "row"), None, None),
        P(("cfg", "row"), "col", None, None, None),
        P(("cfg", "row"), None, None),
        P(("cfg", "row"), None, None),
        P(("cfg", "row"), None, None),
        P(("cfg", "row"), None, None),
    )
    out_specs = (
        P(("cfg", "row"), "col", None, None, None),
        P(("cfg", "row"), None),
        P(("cfg", "row"), "col", None, None, None),
        P(("cfg", "row"), None, None),
        P(("cfg", "row"), None),
    )
    def body(*args):
        if fits_kernel(mesh, *args):
            return on_device_kernel(*args)
        return on_device(*args)

    return jax.shard_map(
        body, mesh=mesh, in_specs=in_specs, out_specs=out_specs, check_vma=False
    )
```

```python
import functools

import jax
import jax.numpy as jnp
from jax import lax
from jax.experimental import pallas as pl
from jax.experimental.pallas import tpu as pltpu
from jax.sharding import PartitionSpec as P

PRECISE = lax.Precision.HIGHEST


def densify(onehot_table, panel):
    spread = jnp.einsum("kqg,kqbn->gbkn", onehot_table, panel, preferred_element_type=jnp.float32)
    return spread.astype(jnp.bfloat16)


def on_device(
    sigma_top, par_panel, par_list, child_panel, child_top, child_list, par_inv, child_inv
):
    col_group = lax.axis_index("col")
    n_parents = par_panel.shape[0]
    n_children = child_panel.shape[0]
    block_width = par_panel.shape[-1]
    n_groups = par_list.shape[1]
    group_blocks = sigma_top.shape[1] // block_width
    total_blocks = n_groups * group_blocks
    slot_count = par_list.shape[2]
    child_count = child_list.shape[2]
    n_panels = n_parents + n_children
    parent_of = jnp.arange(n_children, dtype=jnp.int32) // 2
    par_here = lax.dynamic_index_in_dim(par_list, col_group, 1, keepdims=False)
    child_here = lax.dynamic_index_in_dim(child_list, col_group, 1, keepdims=False)
    child_local = jnp.take_along_axis(par_here[parent_of], child_here, axis=1)
    block_grid = jnp.arange(group_blocks, dtype=jnp.int32)
    par_onehot = (par_here[:, :, None] == block_grid).astype(jnp.bfloat16)
    child_onehot = (child_local[:, :, None] == block_grid).astype(jnp.bfloat16)
    dense_panels = jnp.concatenate(
        [densify(par_onehot, par_panel[:, 0]), densify(child_onehot, child_panel[:, 0])], axis=2
    )
    dense_panels = dense_panels.reshape(group_blocks * block_width, n_panels * block_width)
    products = jnp.dot(
        lax.all_gather(sigma_top, "row", axis=0, tiled=True),
        dense_panels,
        preferred_element_type=jnp.float32,
    ).astype(jnp.bfloat16)
    product_blocks = products.reshape(total_blocks, block_width, n_panels, block_width)
    offsets = (jnp.arange(n_groups, dtype=jnp.int32) * group_blocks)[:, None]
    par_blocks = par_list + offsets[None]
    child_blocks = jnp.take_along_axis(par_blocks[parent_of], child_list, axis=2)

    def pick_blocks(block_index, column):
        found_rows = jnp.take(product_blocks, block_index.reshape(-1), axis=0)
        return lax.dynamic_index_in_dim(found_rows, column, 2, keepdims=False)

    par_partial = jax.vmap(pick_blocks)(par_blocks, jnp.arange(n_parents, dtype=jnp.int32))
    par_partial = par_partial.reshape(n_parents, n_groups, slot_count, block_width, block_width)
    child_partial = jax.vmap(pick_blocks)(
        child_blocks, n_parents + jnp.arange(n_children, dtype=jnp.int32)
    )
    child_partial = child_partial.reshape(
        n_children, n_groups, child_count, block_width, block_width
    )
    par_gram = jnp.einsum("pji,pjk->pik", par_inv, par_inv, precision=PRECISE)
    child_gram = jnp.einsum("cji,cjk->cik", child_inv, child_inv, precision=PRECISE)
    top_wide = child_top.astype(jnp.float32)
    par_recv, child_recv = (
        lax.all_to_all(par_partial, "col", split_axis=1, concat_axis=1, tiled=True),
        lax.all_to_all(child_partial, "col", split_axis=1, concat_axis=1, tiled=True),
    )
    par_sum = jnp.sum(par_recv.astype(jnp.float32), axis=1, keepdims=True)
    child_sum = jnp.sum(child_recv.astype(jnp.float32), axis=1, keepdims=True)
    par_column = (-par_sum).astype(jnp.bfloat16)
    par_col_wide = par_column[:, 0].astype(jnp.float32)
    parent_sel = jnp.take_along_axis(par_col_wide[parent_of], child_here[:, :, None, None], axis=1)
    upper_rows = child_sum[:, 0] + jnp.einsum(
        "csbk,ckn->csbn", parent_sel, top_wide, precision=PRECISE
    )
    child_column = (-upper_rows).astype(jnp.bfloat16)[:, None]
    child_pan_wide = child_panel[:, 0].astype(jnp.float32)
    par_piece = jnp.einsum(
        "pqki,pqkn->pin", par_panel[:, 0].astype(jnp.float32), par_col_wide, precision=PRECISE
    )
    row_piece = jnp.einsum("cski,cskn->cin", parent_sel, child_pan_wide, precision=PRECISE)
    child_piece = jnp.einsum(
        "cski,cskn->cin", child_pan_wide, child_column[:, 0].astype(jnp.float32), precision=PRECISE
    )
    par_total, row_total = lax.psum((par_piece, row_piece), "col")
    par_cov = par_gram - par_total
    parent_rows = row_total + jnp.einsum(
        "cik,ckn->cin", par_cov[parent_of], top_wide, precision=PRECISE
    )
    child_total = lax.psum(child_piece.astype(jnp.bfloat16), "col").astype(jnp.float32)
    child_cov = (
        child_gram
        - child_total
        + jnp.einsum("cki,ckn->cin", top_wide, parent_rows, precision=PRECISE)
    )
    par_var = jnp.diagonal(par_cov, axis1=1, axis2=2)
    child_row = (-parent_rows).astype(jnp.bfloat16)
    child_var = jnp.diagonal(child_cov, axis1=1, axis2=2)
    return (par_column, par_var, child_column, child_row, child_var)


ROWS = 4
COLS = 4
LANES = 128


def transposed_dot(a, b, precision=None):
    return lax.dot_general(
        a, b, (((0,), (0,)), ((), ())), preferred_element_type=jnp.float32, precision=precision
    )


def fused_kernel(
    slots,
    picks,
    kids,
    sig_hbm,
    ppan_hbm,
    cpan_hbm,
    top_hbm,
    pinv_hbm,
    cinv_hbm,
    par_s,
    child_s,
    pcol,
    pvar,
    ccol,
    crow,
    cvar,
    pan_all,
    own_part,
    sib_part,
    pair_sum,
    z_recv,
    x_recv,
    list_all,
    dense,
    dense_out,
    tail_recv,
    kid_recv,
    sig,
    top,
    pinv,
    cinv,
    table,
    local_sem,
    in_send,
    in_recv,
    lst_send,
    lst_recv,
    sib_send,
    sib_recv,
    z_send,
    z_recv_sem,
    x_send,
    x_recv_sem,
    tail_send,
    tail_recv_sem,
    kid_send,
    kid_recv_sem,
):
    width = LANES
    blocks = slots + kids * picks
    z = lax.axis_index("row")
    col = lax.axis_index("col")
    core = lax.rem(col, 2)
    xpos = lax.div(col, 2)
    chip = xpos * 2
    sibling = chip + 1 - core
    across = (1 - xpos) * 2 + core

    def remote(src, dst, send, recv, row, column):
        return pltpu.make_async_remote_copy(
            src_ref=src,
            dst_ref=dst,
            send_sem=send,
            recv_sem=recv,
            device_id={"row": row, "col": column},
            device_id_type=pl.DeviceIdType.MESH,
        )

    def visit(t):
        p = jnp.int32(0)
        for zz in range(ROWS):
            nearest = sorted(range(ROWS), key=lambda q: (abs(q - zz), (q < zz) == (zz >= 2)))
            for tt in range(ROWS):
                p = jnp.where((z == zz) & (t == tt), nearest[tt], p)
        return p

    bounds = ((0, slots), (slots, kids * picks))

    def panel_part(p, part):
        first, count = bounds[part]
        return pan_all.at[p, pl.ds(first, count)]

    loads = [
        pltpu.make_async_copy(src, dst, local_sem.at[i])
        for i, (src, dst) in enumerate(
            (
                (ppan_hbm, panel_part(z, 0)),
                (cpan_hbm, panel_part(z, 1)),
                (sig_hbm, sig),
                (top_hbm, top),
                (pinv_hbm, pinv),
                (cinv_hbm, cinv),
            )
        )
    ]
    for load in loads:
        load.start()

    barrier = pltpu.get_barrier_semaphore()
    for step in range(1, ROWS):
        for k in range(2):
            pl.semaphore_signal(
                barrier,
                inc=1,
                device_id={"row": lax.rem(z + step, ROWS), "col": chip + k},
                device_id_type=pl.DeviceIdType.MESH,
            )
    pl.semaphore_signal(
        barrier, inc=1, device_id={"row": z, "col": sibling}, device_id_type=pl.DeviceIdType.MESH
    )
    for k in range(2):
        pl.semaphore_signal(
            barrier,
            inc=1,
            device_id={"row": z, "col": (1 - xpos) * 2 + k},
            device_id_type=pl.DeviceIdType.MESH,
        )
    table[...] = jnp.zeros_like(table)
    for g in range(COLS):
        for q in range(slots):
            value = par_s[0, g, q].astype(jnp.float32)
            table[g, pl.ds(q, 1), :] = jnp.full((1, width), value, jnp.float32)
        for kid in range(kids):
            for pick in range(picks):
                slot = child_s[kid, g, pick]
                place = par_s[0, g, pick]
                for q in range(pick + 1, slots - picks + pick + 1):
                    place = jnp.where(slot == q, par_s[0, g, q], place)
                value = place.astype(jnp.float32)
                table[g, pl.ds(slots + kid * picks + pick, 1), :] = jnp.full(
                    (1, width), value, jnp.float32
                )
    list_all[z] = table[...].astype(jnp.bfloat16)
    pl.semaphore_wait(barrier, 2 * ROWS + 1)

    def list_copy(step):
        target = lax.rem(z + step, ROWS)
        return remote(
            list_all.at[z], list_all.at[z], lst_send.at[target], lst_recv.at[z], target, col
        )

    def list_arrival(p):
        return remote(list_all.at[p], list_all.at[p], lst_send.at[p], lst_recv.at[p], p, col)

    def forward(p, part, up):
        return remote(
            panel_part(p, part),
            panel_part(p, part),
            in_send.at[up, p, part],
            in_recv.at[p, part],
            z + 1 if up else z - 1,
            col,
        )

    def send_own(part):
        @pl.when(z < ROWS - 1)
        def _():
            forward(z, part, 1).start()

        @pl.when(z > 0)
        def _():
            forward(z, part, 0).start()

    for step in range(1, ROWS):
        list_copy(step).start()
    loads[0].wait()
    send_own(0)
    for load in loads[1:]:
        load.wait()

    def cut(ref, index, part):
        first, count = bounds[part]
        return ref.at[index, pl.ds(first, count)]

    def sib_copy(p, part):
        slot = lax.div(p, 2)
        return remote(
            cut(own_part, p, part),
            cut(sib_part, slot, part),
            sib_send.at[slot, part],
            sib_recv.at[slot, part],
            z,
            sibling,
        )

    def z_copy(p, part):
        slot = lax.div(p, 2)
        here = lax.div(z, 2)
        return remote(
            cut(pair_sum, slot, part),
            cut(z_recv, here, part),
            z_send.at[slot, part],
            z_recv_sem.at[here, part],
            p,
            chip + lax.rem(z, 2),
        )

    def z_arrival(slot, part):
        return remote(
            cut(pair_sum, slot, part),
            cut(z_recv, slot, part),
            z_send.at[slot, part],
            z_recv_sem.at[slot, part],
            core + 2 * slot,
            chip + lax.rem(z, 2),
        )

    def x_copy(part):
        first, count = bounds[part]
        return remote(
            cut(z_recv, 1 - xpos, part),
            x_recv.at[pl.ds(first, count)],
            x_send.at[part],
            x_recv_sem.at[part],
            z,
            across,
        )

    def send_across(part):
        @pl.when(core + 2 * (1 - xpos) != z)
        def _():
            z_arrival(1 - xpos, part).wait_recv()

        x_copy(part).start()

    def take_across(part):
        @pl.when(core + 2 * xpos != z)
        def _():
            z_arrival(xpos, part).wait_recv()

        x_copy(part).wait_recv()

    group_blocks = sig.shape[1] // width
    spans = [(q, group_blocks - slots + q + 1) for q in range(slots)]
    spans += [
        (s, group_blocks - picks + s + 1) for _ in range(kids) for s in range(picks)
    ]
    panel_of = [0] * slots + [1 + kid for kid in range(kids) for _ in range(picks)]

    def places(rows):
        rows = rows.astype(jnp.float32)
        return [jnp.broadcast_to(rows[e : e + 1], (width, width)) for e in range(blocks)]

    def compute(p, part):
        first_entry, count = bounds[part]
        mine = range(first_entry, first_entry + count)
        panels = sorted({panel_of[e] for e in mine})
        low, span = panels[0], len(panels)
        at = places(list_all[p, col])
        for panel in panels:
            entries = [e for e in mine if panel_of[e] == panel]
            for b in range(group_blocks):
                value = jnp.zeros((width, width), jnp.float32)
                for e in entries:
                    if spans[e][0] <= b < spans[e][1]:
                        value = jnp.where(at[e] == b, pan_all[p, e].astype(jnp.float32), value)
                dense[pl.ds(b * width, width), pl.ds(panel * width, width)] = value.astype(
                    jnp.bfloat16
                )
        lanes = pl.ds(low * width, span * width)
        dense_out[:, lanes] = jnp.dot(
            sig[...], dense[:, lanes], preferred_element_type=jnp.float32
        )
        at = places(list_all[p, z])
        for e in mine:
            first, end = spans[e]
            lane = pl.ds(panel_of[e] * width, width)
            value = dense_out[pl.ds(first * width, width), lane]
            for b in range(first + 1, end):
                value = jnp.where(at[e] == b, dense_out[pl.ds(b * width, width), lane], value)
            own_part[p, e] = value.astype(jnp.bfloat16)

    def combine(p, part):
        first, count = bounds[part]
        slot = lax.div(p, 2)
        sib_copy(p, part).wait_recv()

        @pl.loop(first, first + count)
        def _(b):
            total = own_part[p, b].astype(jnp.float32) + sib_part[slot, b].astype(jnp.float32)
            pair_sum[slot, b] = total.astype(jnp.bfloat16)

        @pl.when(p == z)
        def _():
            z_recv[slot, pl.ds(first, count)] = pair_sum[slot, pl.ds(first, count)]

        @pl.when(p != z)
        def _():
            z_copy(p, part).start()

    def stage(part):
        @pl.loop(0, ROWS + 1)
        def _(t):
            @pl.when(t < ROWS)
            def _():
                p = visit(t)

                @pl.when(p != z)
                def _():
                    forward(p, part, 0).wait_recv()

                    @pl.when((p < z) & (z < ROWS - 1))
                    def _():
                        forward(p, part, 1).start()

                    @pl.when((p > z) & (z > 0))
                    def _():
                        forward(p, part, 0).start()

                    if part == 0:
                        list_arrival(p).wait_recv()

                if part == 0:

                    @pl.when(t == 1)
                    def _():
                        send_own(1)

                compute(p, part)

                @pl.when(lax.rem(p, 2) != core)
                def _():
                    sib_copy(p, part).start()

            if part == 1:

                @pl.when(t == ROWS)
                def _():
                    send_across(0)

            @pl.when(t > 0)
            def _():
                p = visit(t - 1)

                @pl.when(lax.rem(p, 2) == core)
                def _():
                    combine(p, part)

    stage(0)
    stage(1)

    precise = lax.Precision.HIGHEST
    gram = transposed_dot(pinv[...], pinv[...], precise)
    wide_top = [top[kid].astype(jnp.float32) for kid in range(kids)]
    gram_top = [
        jnp.dot(gram, wide, precision=precise, preferred_element_type=jnp.float32)
        for wide in wide_top
    ]

    def spread(buffer, send, recv, source, target):
        return remote(
            buffer.at[source], buffer.at[source], send.at[target], recv.at[source], z, target
        )

    def send_to_columns(buffer, send, recv):
        for step in range(1, COLS):
            spread(buffer, send, recv, col, lax.rem(col + step, COLS)).start()

    def take_from_columns(buffer, send, recv):
        for step in range(1, COLS):
            source = lax.rem(col + step, COLS)
            spread(buffer, send, recv, source, source).wait_recv()

    take_across(0)
    par_diag = jnp.zeros((1, width), jnp.float32)
    for q in range(slots):
        total = z_recv[xpos, q].astype(jnp.float32) + x_recv[q].astype(jnp.float32)
        column = (-total).astype(jnp.bfloat16)
        pcol[q] = column
        par_diag += jnp.sum(
            pan_all[z, q].astype(jnp.float32) * column.astype(jnp.float32), axis=0, keepdims=True
        )
    par_piece = transposed_dot(
        pan_all[z, pl.ds(0, slots)].reshape(slots * width, width),
        pcol[...].reshape(slots * width, width),
    )
    lifted = []
    for kid in range(kids):
        selected = []
        for s in range(picks):
            slot = jnp.full((width, width), child_s[kid, col, s], jnp.int32)
            value = pcol[s].astype(jnp.float32)
            for q in range(s + 1, slots - picks + s + 1):
                value = jnp.where(slot == q, pcol[q].astype(jnp.float32), value)
            selected.append(value.astype(jnp.bfloat16))
        chosen = jnp.concatenate(selected, axis=0)
        piece = transposed_dot(
            chosen,
            pan_all[z, pl.ds(slots + kid * picks, picks)].reshape(picks * width, width),
        )
        piece = piece - jnp.dot(
            par_piece, wide_top[kid], precision=precise, preferred_element_type=jnp.float32
        )
        tail_recv[col, pl.ds(kid * width, width)] = piece.astype(jnp.bfloat16)
        lifted.append(jnp.dot(chosen, top[kid], preferred_element_type=jnp.float32))
    send_across(1)
    send_to_columns(tail_recv, tail_send, tail_recv_sem)

    take_across(1)
    kid_diags = []
    for kid in range(kids):
        kid_diag = jnp.zeros((1, width), jnp.float32)
        for s in range(picks):
            at = kid * picks + s
            upper = (
                z_recv[xpos, slots + at].astype(jnp.float32)
                + x_recv[slots + at].astype(jnp.float32)
                + lifted[kid][s * width : (s + 1) * width]
            )
            column = (-upper).astype(jnp.bfloat16)
            ccol[at] = column
            kid_diag += jnp.sum(
                pan_all[z, slots + at].astype(jnp.float32) * column.astype(jnp.float32),
                axis=0,
                keepdims=True,
            )
        kid_diags.append(kid_diag)
    kid_diags.append(jnp.broadcast_to(par_diag, (8 - kids, width)))
    kid_recv[col] = jnp.concatenate(kid_diags, axis=0)
    send_to_columns(kid_recv, kid_send, kid_recv_sem)

    take_from_columns(tail_recv, tail_send, tail_recv_sem)
    par_squares = jnp.sum(pinv[...] * pinv[...], axis=0, keepdims=True)
    known = []
    for kid in range(kids):
        part = [
            tail_recv[c, pl.ds(kid * width, width)].astype(jnp.float32) for c in range(COLS)
        ]
        rows = part[0] + part[1] + part[2] + part[3] + gram_top[kid]
        crow[kid] = (-rows).astype(jnp.bfloat16)
        inv = cinv[kid]
        known.append(
            jnp.sum(inv * inv, axis=0, keepdims=True)
            + jnp.sum(wide_top[kid] * rows, axis=0, keepdims=True)
        )
    take_from_columns(kid_recv, kid_send, kid_recv_sem)
    kid_total = kid_recv[0] + kid_recv[1] + kid_recv[2] + kid_recv[3]
    pvar[...] = par_squares - kid_total[kids : kids + 1]
    for kid in range(kids):
        cvar[pl.ds(kid, 1), :] = known[kid] - kid_total[kid : kid + 1]

    for step in range(1, ROWS):
        list_copy(step).wait_send()
    for step in range(1, COLS):
        target = lax.rem(col + step, COLS)
        spread(tail_recv, tail_send, tail_recv_sem, col, target).wait_send()
        spread(kid_recv, kid_send, kid_recv_sem, col, target).wait_send()
    for part in range(2):
        for p in range(ROWS):

            @pl.when((p <= z) & (z < ROWS - 1))
            def _():
                forward(p, part, 1).wait_send()

            @pl.when((p >= z) & (z > 0))
            def _():
                forward(p, part, 0).wait_send()

        for slot in range(2):
            sib_copy(1 - core + 2 * slot, part).wait_send()

            @pl.when(core + 2 * slot != z)
            def _():
                z_copy(core + 2 * slot, part).wait_send()

        x_copy(part).wait_send()


def fits_kernel(
    mesh, sigma_top, par_panel, par_list, child_panel, child_top, child_list, par_inv, child_inv
):
    groups = par_list.shape[1]
    order = sigma_top.shape[1]
    return (
        mesh.shape["row"] == ROWS
        and mesh.shape["col"] == COLS
        and groups == COLS
        and sigma_top.shape[0] == order
        and par_panel.shape[0] == 1
        and par_panel.shape[-1] == LANES
        and child_panel.shape[0] <= 7
        and order * order <= 1 << 22
    )


def on_device_kernel(
    sigma_top, par_panel, par_list, child_panel, child_top, child_list, par_inv, child_inv
):
    slots = par_panel.shape[2]
    kids, _, picks = child_panel.shape[:3]
    width = LANES
    blocks = slots + kids * picks

    group_blocks = sigma_top.shape[1] // width
    pad = -blocks % 16
    bf16, f32 = jnp.bfloat16, jnp.float32
    vmem = pl.BlockSpec(memory_space=pltpu.VMEM)
    smem = pl.BlockSpec(memory_space=pltpu.SMEM)
    hbm = pl.BlockSpec(memory_space=pltpu.HBM)
    dma = pltpu.SemaphoreType.DMA
    outs = pl.pallas_call(
        functools.partial(fused_kernel, slots, picks, kids),
        out_shape=(
            jax.ShapeDtypeStruct((slots, width, width), bf16),
            jax.ShapeDtypeStruct((1, width), f32),
            jax.ShapeDtypeStruct((kids * picks, width, width), bf16),
            jax.ShapeDtypeStruct((kids, width, width), bf16),
            jax.ShapeDtypeStruct((kids, width), f32),
        ),
        in_specs=[hbm] * 6 + [smem] * 2,
        out_specs=[vmem] * 5,
        scratch_shapes=[
            pltpu.VMEM((ROWS, blocks, width, width), bf16),
            pltpu.VMEM((ROWS, blocks, width, width), bf16),
            pltpu.VMEM((2, blocks, width, width), bf16),
            pltpu.VMEM((2, blocks, width, width), bf16),
            pltpu.VMEM((2, blocks, width, width), bf16),
            pltpu.VMEM((blocks, width, width), bf16),
            pltpu.VMEM((ROWS, COLS, blocks + pad, LANES), bf16),
            pltpu.VMEM((group_blocks * width, (1 + kids) * width), bf16),
            pltpu.VMEM((group_blocks * width, (1 + kids) * width), f32),
            pltpu.VMEM((COLS, kids * width, width), bf16),
            pltpu.VMEM((COLS, 8, width), f32),
            pltpu.VMEM(sigma_top.shape, bf16),
            pltpu.VMEM(child_top.shape, bf16),
            pltpu.VMEM((width, width), f32),
            pltpu.VMEM(child_inv.shape, f32),
            pltpu.VMEM((COLS, blocks + pad, LANES), f32),
            dma((6,)),
            dma((2, ROWS, 2)),
            dma((ROWS, 2)),
            dma((ROWS,)),
            dma((ROWS,)),
            dma((2, 2)),
            dma((2, 2)),
            dma((2, 2)),
            dma((2, 2)),
            dma((2,)),
            dma((2,)),
            dma((COLS,)),
            dma((COLS,)),
            dma((COLS,)),
            dma((COLS,)),
        ],
        compiler_params=pltpu.CompilerParams(
            collective_id=0, has_side_effects=True, vmem_limit_bytes=60 * 1024 * 1024
        ),
    )(
        sigma_top,
        par_panel.reshape(slots, width, width),
        child_panel.reshape(kids * picks, width, width),
        child_top,
        par_inv.reshape(width, width),
        child_inv,
        par_list,
        child_list,
    )
    pcol, pvar, ccol, crow, cvar = outs
    return (
        pcol.reshape(par_panel.shape),
        pvar,
        ccol.reshape(child_panel.shape),
        crow,
        cvar,
    )


def solution(mesh):
    in_specs = (
        P(("cfg", "row"), "col"),
        P(("cfg", "row"), "col", None, None, None),
        P(("cfg", "row"), None, None),
        P(("cfg", "row"), "col", None, None, None),
        P(("cfg", "row"), None, None),
        P(("cfg", "row"), None, None),
        P(("cfg", "row"), None, None),
        P(("cfg", "row"), None, None),
    )
    out_specs = (
        P(("cfg", "row"), "col", None, None, None),
        P(("cfg", "row"), None),
        P(("cfg", "row"), "col", None, None, None),
        P(("cfg", "row"), None, None),
        P(("cfg", "row"), None),
    )
    def body(*args):
        if fits_kernel(mesh, *args):
            return on_device_kernel(*args)
        return on_device(*args)

    return jax.shard_map(
        body, mesh=mesh, in_specs=in_specs, out_specs=out_specs, check_vma=False
    )
```

```python
import functools

import jax
import jax.numpy as jnp
from jax import lax
from jax.experimental import pallas as pl
from jax.experimental.pallas import tpu as pltpu
from jax.sharding import PartitionSpec as P

PRECISE = lax.Precision.HIGHEST


def densify(onehot_table, panel):
    spread = jnp.einsum("kqg,kqbn->gbkn", onehot_table, panel, preferred_element_type=jnp.float32)
    return spread.astype(jnp.bfloat16)


def on_device(
    sigma_top, par_panel, par_list, child_panel, child_top, child_list, par_inv, child_inv
):
    col_group = lax.axis_index("col")
    n_parents = par_panel.shape[0]
    n_children = child_panel.shape[0]
    block_width = par_panel.shape[-1]
    n_groups = par_list.shape[1]
    group_blocks = sigma_top.shape[1] // block_width
    total_blocks = n_groups * group_blocks
    slot_count = par_list.shape[2]
    child_count = child_list.shape[2]
    n_panels = n_parents + n_children
    parent_of = jnp.arange(n_children, dtype=jnp.int32) // 2
    par_here = lax.dynamic_index_in_dim(par_list, col_group, 1, keepdims=False)
    child_here = lax.dynamic_index_in_dim(child_list, col_group, 1, keepdims=False)
    child_local = jnp.take_along_axis(par_here[parent_of], child_here, axis=1)
    block_grid = jnp.arange(group_blocks, dtype=jnp.int32)
    par_onehot = (par_here[:, :, None] == block_grid).astype(jnp.bfloat16)
    child_onehot = (child_local[:, :, None] == block_grid).astype(jnp.bfloat16)
    dense_panels = jnp.concatenate(
        [densify(par_onehot, par_panel[:, 0]), densify(child_onehot, child_panel[:, 0])], axis=2
    )
    dense_panels = dense_panels.reshape(group_blocks * block_width, n_panels * block_width)
    products = jnp.dot(
        lax.all_gather(sigma_top, "row", axis=0, tiled=True),
        dense_panels,
        preferred_element_type=jnp.float32,
    ).astype(jnp.bfloat16)
    product_blocks = products.reshape(total_blocks, block_width, n_panels, block_width)
    offsets = (jnp.arange(n_groups, dtype=jnp.int32) * group_blocks)[:, None]
    par_blocks = par_list + offsets[None]
    child_blocks = jnp.take_along_axis(par_blocks[parent_of], child_list, axis=2)

    def pick_blocks(block_index, column):
        found_rows = jnp.take(product_blocks, block_index.reshape(-1), axis=0)
        return lax.dynamic_index_in_dim(found_rows, column, 2, keepdims=False)

    par_partial = jax.vmap(pick_blocks)(par_blocks, jnp.arange(n_parents, dtype=jnp.int32))
    par_partial = par_partial.reshape(n_parents, n_groups, slot_count, block_width, block_width)
    child_partial = jax.vmap(pick_blocks)(
        child_blocks, n_parents + jnp.arange(n_children, dtype=jnp.int32)
    )
    child_partial = child_partial.reshape(
        n_children, n_groups, child_count, block_width, block_width
    )
    par_gram = jnp.einsum("pji,pjk->pik", par_inv, par_inv, precision=PRECISE)
    child_gram = jnp.einsum("cji,cjk->cik", child_inv, child_inv, precision=PRECISE)
    top_wide = child_top.astype(jnp.float32)
    par_recv, child_recv = (
        lax.all_to_all(par_partial, "col", split_axis=1, concat_axis=1, tiled=True),
        lax.all_to_all(child_partial, "col", split_axis=1, concat_axis=1, tiled=True),
    )
    par_sum = jnp.sum(par_recv.astype(jnp.float32), axis=1, keepdims=True)
    child_sum = jnp.sum(child_recv.astype(jnp.float32), axis=1, keepdims=True)
    par_column = (-par_sum).astype(jnp.bfloat16)
    par_col_wide = par_column[:, 0].astype(jnp.float32)
    parent_sel = jnp.take_along_axis(par_col_wide[parent_of], child_here[:, :, None, None], axis=1)
    upper_rows = child_sum[:, 0] + jnp.einsum(
        "csbk,ckn->csbn", parent_sel, top_wide, precision=PRECISE
    )
    child_column = (-upper_rows).astype(jnp.bfloat16)[:, None]
    child_pan_wide = child_panel[:, 0].astype(jnp.float32)
    par_piece = jnp.einsum(
        "pqki,pqkn->pin", par_panel[:, 0].astype(jnp.float32), par_col_wide, precision=PRECISE
    )
    row_piece = jnp.einsum("cski,cskn->cin", parent_sel, child_pan_wide, precision=PRECISE)
    child_piece = jnp.einsum(
        "cski,cskn->cin", child_pan_wide, child_column[:, 0].astype(jnp.float32), precision=PRECISE
    )
    par_total, row_total = lax.psum((par_piece, row_piece), "col")
    par_cov = par_gram - par_total
    parent_rows = row_total + jnp.einsum(
        "cik,ckn->cin", par_cov[parent_of], top_wide, precision=PRECISE
    )
    child_total = lax.psum(child_piece.astype(jnp.bfloat16), "col").astype(jnp.float32)
    child_cov = (
        child_gram
        - child_total
        + jnp.einsum("cki,ckn->cin", top_wide, parent_rows, precision=PRECISE)
    )
    par_var = jnp.diagonal(par_cov, axis1=1, axis2=2)
    child_row = (-parent_rows).astype(jnp.bfloat16)
    child_var = jnp.diagonal(child_cov, axis1=1, axis2=2)
    return (par_column, par_var, child_column, child_row, child_var)


ROWS = 4
COLS = 4
LANES = 128


def transposed_dot(a, b, precision=None):
    return lax.dot_general(
        a, b, (((0,), (0,)), ((), ())), preferred_element_type=jnp.float32, precision=precision
    )


def fused_kernel(
    slots,
    picks,
    kids,
    sig_hbm,
    ppan_hbm,
    cpan_hbm,
    top_hbm,
    pinv_hbm,
    cinv_hbm,
    par_s,
    child_s,
    pcol,
    pvar,
    ccol,
    crow,
    cvar,
    pan_all,
    own_part,
    sib_part,
    pair_sum,
    z_recv,
    x_recv,
    list_all,
    dense,
    dense_out,
    tail_recv,
    kid_recv,
    sig,
    top,
    pinv,
    cinv,
    table,
    local_sem,
    in_send,
    in_recv,
    lst_send,
    lst_recv,
    sib_send,
    sib_recv,
    z_send,
    z_recv_sem,
    x_send,
    x_recv_sem,
    tail_send,
    tail_recv_sem,
    kid_send,
    kid_recv_sem,
):
    width = LANES
    blocks = slots + kids * picks
    z = lax.axis_index("row")
    col = lax.axis_index("col")
    core = lax.rem(col, 2)
    xpos = lax.div(col, 2)
    chip = xpos * 2
    sibling = chip + 1 - core
    across = (1 - xpos) * 2 + core

    def remote(src, dst, send, recv, row, column):
        return pltpu.make_async_remote_copy(
            src_ref=src,
            dst_ref=dst,
            send_sem=send,
            recv_sem=recv,
            device_id={"row": row, "col": column},
            device_id_type=pl.DeviceIdType.MESH,
        )

    def visit(t):
        p = jnp.int32(0)
        for zz in range(ROWS):
            nearest = sorted(range(ROWS), key=lambda q: (abs(q - zz), (q < zz) == (zz >= 2)))
            for tt in range(ROWS):
                p = jnp.where((z == zz) & (t == tt), nearest[tt], p)
        return p

    bounds = ((0, slots), (slots, kids * picks))

    def panel_part(p, part):
        first, count = bounds[part]
        return pan_all.at[p, pl.ds(first, count)]

    loads = [
        pltpu.make_async_copy(src, dst, local_sem.at[i])
        for i, (src, dst) in enumerate(
            (
                (ppan_hbm, panel_part(z, 0)),
                (cpan_hbm, panel_part(z, 1)),
                (sig_hbm, sig),
                (top_hbm, top),
                (pinv_hbm, pinv),
                (cinv_hbm, cinv),
            )
        )
    ]
    for load in loads:
        load.start()

    barrier = pltpu.get_barrier_semaphore()
    for step in range(1, ROWS):
        for k in range(2):
            pl.semaphore_signal(
                barrier,
                inc=1,
                device_id={"row": lax.rem(z + step, ROWS), "col": chip + k},
                device_id_type=pl.DeviceIdType.MESH,
            )
    pl.semaphore_signal(
        barrier, inc=1, device_id={"row": z, "col": sibling}, device_id_type=pl.DeviceIdType.MESH
    )
    for k in range(2):
        pl.semaphore_signal(
            barrier,
            inc=1,
            device_id={"row": z, "col": (1 - xpos) * 2 + k},
            device_id_type=pl.DeviceIdType.MESH,
        )
    table[...] = jnp.zeros_like(table)
    for g in range(COLS):
        for q in range(slots):
            value = par_s[0, g, q].astype(jnp.float32)
            table[g, pl.ds(q, 1), :] = jnp.full((1, width), value, jnp.float32)
        for kid in range(kids):
            for pick in range(picks):
                slot = child_s[kid, g, pick]
                place = par_s[0, g, pick]
                for q in range(pick + 1, slots - picks + pick + 1):
                    place = jnp.where(slot == q, par_s[0, g, q], place)
                value = place.astype(jnp.float32)
                table[g, pl.ds(slots + kid * picks + pick, 1), :] = jnp.full(
                    (1, width), value, jnp.float32
                )
    list_all[z] = table[...].astype(jnp.bfloat16)
    pl.semaphore_wait(barrier, 2 * ROWS + 1)

    def list_copy(step):
        target = lax.rem(z + step, ROWS)
        return remote(
            list_all.at[z], list_all.at[z], lst_send.at[target], lst_recv.at[z], target, col
        )

    def list_arrival(p):
        return remote(list_all.at[p], list_all.at[p], lst_send.at[p], lst_recv.at[p], p, col)

    def forward(p, part, up):
        return remote(
            panel_part(p, part),
            panel_part(p, part),
            in_send.at[up, p, part],
            in_recv.at[p, part],
            z + 1 if up else z - 1,
            col,
        )

    def send_own(part):
        @pl.when(z < ROWS - 1)
        def _():
            forward(z, part, 1).start()

        @pl.when(z > 0)
        def _():
            forward(z, part, 0).start()

    for step in range(1, ROWS):
        list_copy(step).start()
    loads[0].wait()
    send_own(0)
    loads[1].wait()
    send_own(1)
    for load in loads[2:]:
        load.wait()

    def cut(ref, index, part):
        first, count = bounds[part]
        return ref.at[index, pl.ds(first, count)]

    def sib_copy(p, part):
        slot = lax.div(p, 2)
        return remote(
            cut(own_part, p, part),
            cut(sib_part, slot, part),
            sib_send.at[slot, part],
            sib_recv.at[slot, part],
            z,
            sibling,
        )

    def z_copy(p, part):
        slot = lax.div(p, 2)
        here = lax.div(z, 2)
        return remote(
            cut(pair_sum, slot, part),
            cut(z_recv, here, part),
            z_send.at[slot, part],
            z_recv_sem.at[here, part],
            p,
            chip + lax.rem(z, 2),
        )

    def z_arrival(slot, part):
        return remote(
            cut(pair_sum, slot, part),
            cut(z_recv, slot, part),
            z_send.at[slot, part],
            z_recv_sem.at[slot, part],
            core + 2 * slot,
            chip + lax.rem(z, 2),
        )

    def x_copy(part):
        first, count = bounds[part]
        return remote(
            cut(z_recv, 1 - xpos, part),
            x_recv.at[pl.ds(first, count)],
            x_send.at[part],
            x_recv_sem.at[part],
            z,
            across,
        )

    def send_across(part):
        @pl.when(core + 2 * (1 - xpos) != z)
        def _():
            z_arrival(1 - xpos, part).wait_recv()

        x_copy(part).start()

    def take_across(part):
        @pl.when(core + 2 * xpos != z)
        def _():
            z_arrival(xpos, part).wait_recv()

        x_copy(part).wait_recv()

    group_blocks = sig.shape[1] // width
    spans = [(q, group_blocks - slots + q + 1) for q in range(slots)]
    spans += [
        (s, group_blocks - picks + s + 1) for _ in range(kids) for s in range(picks)
    ]
    panel_of = [0] * slots + [1 + kid for kid in range(kids) for _ in range(picks)]

    def places(rows):
        rows = rows.astype(jnp.float32)
        return [jnp.broadcast_to(rows[e : e + 1], (width, width)) for e in range(blocks)]

    def compute(p, part):
        first_entry, count = bounds[part]
        mine = range(first_entry, first_entry + count)
        panels = sorted({panel_of[e] for e in mine})
        low, span = panels[0], len(panels)
        at = places(list_all[p, col])
        for panel in panels:
            entries = [e for e in mine if panel_of[e] == panel]
            for b in range(group_blocks):
                value = jnp.zeros((width, width), jnp.float32)
                for e in entries:
                    if spans[e][0] <= b < spans[e][1]:
                        value = jnp.where(at[e] == b, pan_all[p, e].astype(jnp.float32), value)
                dense[pl.ds(b * width, width), pl.ds(panel * width, width)] = value.astype(
                    jnp.bfloat16
                )
        lanes = pl.ds(low * width, span * width)
        dense_out[:, lanes] = jnp.dot(
            sig[...], dense[:, lanes], preferred_element_type=jnp.float32
        )
        at = places(list_all[p, z])
        for e in mine:
            first, end = spans[e]
            lane = pl.ds(panel_of[e] * width, width)
            value = dense_out[pl.ds(first * width, width), lane]
            for b in range(first + 1, end):
                value = jnp.where(at[e] == b, dense_out[pl.ds(b * width, width), lane], value)
            own_part[p, e] = value.astype(jnp.bfloat16)

    def combine(p, part):
        first, count = bounds[part]
        slot = lax.div(p, 2)
        sib_copy(p, part).wait_recv()

        @pl.loop(first, first + count)
        def _(b):
            total = own_part[p, b].astype(jnp.float32) + sib_part[slot, b].astype(jnp.float32)
            pair_sum[slot, b] = total.astype(jnp.bfloat16)

        @pl.when(p == z)
        def _():
            z_recv[slot, pl.ds(first, count)] = pair_sum[slot, pl.ds(first, count)]

        @pl.when(p != z)
        def _():
            z_copy(p, part).start()

    def stage(part):
        @pl.loop(0, ROWS + 1)
        def _(t):
            @pl.when(t < ROWS)
            def _():
                p = visit(t)

                @pl.when(p != z)
                def _():
                    forward(p, part, 0).wait_recv()

                    @pl.when((p < z) & (z < ROWS - 1))
                    def _():
                        forward(p, part, 1).start()

                    @pl.when((p > z) & (z > 0))
                    def _():
                        forward(p, part, 0).start()

                    if part == 0:
                        list_arrival(p).wait_recv()

                compute(p, part)

                @pl.when(lax.rem(p, 2) != core)
                def _():
                    sib_copy(p, part).start()

            if part == 1:

                @pl.when(t == ROWS)
                def _():
                    send_across(0)

            @pl.when(t > 0)
            def _():
                p = visit(t - 1)

                @pl.when(lax.rem(p, 2) == core)
                def _():
                    combine(p, part)

    stage(0)
    stage(1)

    precise = lax.Precision.HIGHEST
    gram = transposed_dot(pinv[...], pinv[...], precise)
    wide_top = [top[kid].astype(jnp.float32) for kid in range(kids)]
    gram_top = [
        jnp.dot(gram, wide, precision=precise, preferred_element_type=jnp.float32)
        for wide in wide_top
    ]

    def spread(buffer, send, recv, source, target):
        return remote(
            buffer.at[source], buffer.at[source], send.at[target], recv.at[source], z, target
        )

    def send_to_columns(buffer, send, recv):
        for step in range(1, COLS):
            spread(buffer, send, recv, col, lax.rem(col + step, COLS)).start()

    def take_from_columns(buffer, send, recv):
        for step in range(1, COLS):
            source = lax.rem(col + step, COLS)
            spread(buffer, send, recv, source, source).wait_recv()

    take_across(0)
    par_diag = jnp.zeros((1, width), jnp.float32)
    for q in range(slots):
        total = z_recv[xpos, q].astype(jnp.float32) + x_recv[q].astype(jnp.float32)
        column = (-total).astype(jnp.bfloat16)
        pcol[q] = column
        par_diag += jnp.sum(
            pan_all[z, q].astype(jnp.float32) * column.astype(jnp.float32), axis=0, keepdims=True
        )
    par_piece = transposed_dot(
        pan_all[z, pl.ds(0, slots)].reshape(slots * width, width),
        pcol[...].reshape(slots * width, width),
    )
    lifted = []
    for kid in range(kids):
        selected = []
        for s in range(picks):
            slot = jnp.full((width, width), child_s[kid, col, s], jnp.int32)
            value = pcol[s].astype(jnp.float32)
            for q in range(s + 1, slots - picks + s + 1):
                value = jnp.where(slot == q, pcol[q].astype(jnp.float32), value)
            selected.append(value.astype(jnp.bfloat16))
        chosen = jnp.concatenate(selected, axis=0)
        piece = transposed_dot(
            chosen,
            pan_all[z, pl.ds(slots + kid * picks, picks)].reshape(picks * width, width),
        )
        piece = piece - jnp.dot(
            par_piece, wide_top[kid], precision=precise, preferred_element_type=jnp.float32
        )
        tail_recv[col, pl.ds(kid * width, width)] = piece.astype(jnp.bfloat16)
        lifted.append(jnp.dot(chosen, top[kid], preferred_element_type=jnp.float32))
    send_across(1)
    send_to_columns(tail_recv, tail_send, tail_recv_sem)

    take_across(1)
    kid_diags = []
    for kid in range(kids):
        kid_diag = jnp.zeros((1, width), jnp.float32)
        for s in range(picks):
            at = kid * picks + s
            upper = (
                z_recv[xpos, slots + at].astype(jnp.float32)
                + x_recv[slots + at].astype(jnp.float32)
                + lifted[kid][s * width : (s + 1) * width]
            )
            column = (-upper).astype(jnp.bfloat16)
            ccol[at] = column
            kid_diag += jnp.sum(
                pan_all[z, slots + at].astype(jnp.float32) * column.astype(jnp.float32),
                axis=0,
                keepdims=True,
            )
        kid_diags.append(kid_diag)
    kid_diags.append(jnp.broadcast_to(par_diag, (8 - kids, width)))
    kid_recv[col] = jnp.concatenate(kid_diags, axis=0)
    send_to_columns(kid_recv, kid_send, kid_recv_sem)

    take_from_columns(tail_recv, tail_send, tail_recv_sem)
    par_squares = jnp.sum(pinv[...] * pinv[...], axis=0, keepdims=True)
    known = []
    for kid in range(kids):
        part = [
            tail_recv[c, pl.ds(kid * width, width)].astype(jnp.float32) for c in range(COLS)
        ]
        rows = part[0] + part[1] + part[2] + part[3] + gram_top[kid]
        crow[kid] = (-rows).astype(jnp.bfloat16)
        inv = cinv[kid]
        known.append(
            jnp.sum(inv * inv, axis=0, keepdims=True)
            + jnp.sum(wide_top[kid] * rows, axis=0, keepdims=True)
        )
    take_from_columns(kid_recv, kid_send, kid_recv_sem)
    kid_total = kid_recv[0] + kid_recv[1] + kid_recv[2] + kid_recv[3]
    pvar[...] = par_squares - kid_total[kids : kids + 1]
    for kid in range(kids):
        cvar[pl.ds(kid, 1), :] = known[kid] - kid_total[kid : kid + 1]

    for step in range(1, ROWS):
        list_copy(step).wait_send()
    for step in range(1, COLS):
        target = lax.rem(col + step, COLS)
        spread(tail_recv, tail_send, tail_recv_sem, col, target).wait_send()
        spread(kid_recv, kid_send, kid_recv_sem, col, target).wait_send()
    for part in range(2):
        for p in range(ROWS):

            @pl.when((p <= z) & (z < ROWS - 1))
            def _():
                forward(p, part, 1).wait_send()

            @pl.when((p >= z) & (z > 0))
            def _():
                forward(p, part, 0).wait_send()

        for slot in range(2):
            sib_copy(1 - core + 2 * slot, part).wait_send()

            @pl.when(core + 2 * slot != z)
            def _():
                z_copy(core + 2 * slot, part).wait_send()

        x_copy(part).wait_send()


def fits_kernel(
    mesh, sigma_top, par_panel, par_list, child_panel, child_top, child_list, par_inv, child_inv
):
    groups = par_list.shape[1]
    order = sigma_top.shape[1]
    return (
        mesh.shape["row"] == ROWS
        and mesh.shape["col"] == COLS
        and groups == COLS
        and sigma_top.shape[0] == order
        and par_panel.shape[0] == 1
        and par_panel.shape[-1] == LANES
        and child_panel.shape[0] <= 7
        and order * order <= 1 << 22
    )


def on_device_kernel(
    sigma_top, par_panel, par_list, child_panel, child_top, child_list, par_inv, child_inv
):
    slots = par_panel.shape[2]
    kids, _, picks = child_panel.shape[:3]
    width = LANES
    blocks = slots + kids * picks

    group_blocks = sigma_top.shape[1] // width
    pad = -blocks % 16
    bf16, f32 = jnp.bfloat16, jnp.float32
    vmem = pl.BlockSpec(memory_space=pltpu.VMEM)
    smem = pl.BlockSpec(memory_space=pltpu.SMEM)
    hbm = pl.BlockSpec(memory_space=pltpu.HBM)
    dma = pltpu.SemaphoreType.DMA
    outs = pl.pallas_call(
        functools.partial(fused_kernel, slots, picks, kids),
        out_shape=(
            jax.ShapeDtypeStruct((slots, width, width), bf16),
            jax.ShapeDtypeStruct((1, width), f32),
            jax.ShapeDtypeStruct((kids * picks, width, width), bf16),
            jax.ShapeDtypeStruct((kids, width, width), bf16),
            jax.ShapeDtypeStruct((kids, width), f32),
        ),
        in_specs=[hbm] * 6 + [smem] * 2,
        out_specs=[vmem] * 5,
        scratch_shapes=[
            pltpu.VMEM((ROWS, blocks, width, width), bf16),
            pltpu.VMEM((ROWS, blocks, width, width), bf16),
            pltpu.VMEM((2, blocks, width, width), bf16),
            pltpu.VMEM((2, blocks, width, width), bf16),
            pltpu.VMEM((2, blocks, width, width), bf16),
            pltpu.VMEM((blocks, width, width), bf16),
            pltpu.VMEM((ROWS, COLS, blocks + pad, LANES), bf16),
            pltpu.VMEM((group_blocks * width, (1 + kids) * width), bf16),
            pltpu.VMEM((group_blocks * width, (1 + kids) * width), f32),
            pltpu.VMEM((COLS, kids * width, width), bf16),
            pltpu.VMEM((COLS, 8, width), f32),
            pltpu.VMEM(sigma_top.shape, bf16),
            pltpu.VMEM(child_top.shape, bf16),
            pltpu.VMEM((width, width), f32),
            pltpu.VMEM(child_inv.shape, f32),
            pltpu.VMEM((COLS, blocks + pad, LANES), f32),
            dma((6,)),
            dma((2, ROWS, 2)),
            dma((ROWS, 2)),
            dma((ROWS,)),
            dma((ROWS,)),
            dma((2, 2)),
            dma((2, 2)),
            dma((2, 2)),
            dma((2, 2)),
            dma((2,)),
            dma((2,)),
            dma((COLS,)),
            dma((COLS,)),
            dma((COLS,)),
            dma((COLS,)),
        ],
        compiler_params=pltpu.CompilerParams(
            collective_id=0, has_side_effects=True, vmem_limit_bytes=60 * 1024 * 1024
        ),
    )(
        sigma_top,
        par_panel.reshape(slots, width, width),
        child_panel.reshape(kids * picks, width, width),
        child_top,
        par_inv.reshape(width, width),
        child_inv,
        par_list,
        child_list,
    )
    pcol, pvar, ccol, crow, cvar = outs
    return (
        pcol.reshape(par_panel.shape),
        pvar,
        ccol.reshape(child_panel.shape),
        crow,
        cvar,
    )


def solution(mesh):
    in_specs = (
        P(("cfg", "row"), "col"),
        P(("cfg", "row"), "col", None, None, None),
        P(("cfg", "row"), None, None),
        P(("cfg", "row"), "col", None, None, None),
        P(("cfg", "row"), None, None),
        P(("cfg", "row"), None, None),
        P(("cfg", "row"), None, None),
        P(("cfg", "row"), None, None),
    )
    out_specs = (
        P(("cfg", "row"), "col", None, None, None),
        P(("cfg", "row"), None),
        P(("cfg", "row"), "col", None, None, None),
        P(("cfg", "row"), None, None),
        P(("cfg", "row"), None),
    )
    def body(*args):
        if fits_kernel(mesh, *args):
            return on_device_kernel(*args)
        return on_device(*args)

    return jax.shard_map(
        body, mesh=mesh, in_specs=in_specs, out_specs=out_specs, check_vma=False
    )
```
